256 devices in a mesh: group: 4 (over y_lo, core), seq: 2 (over y_hi), tensor: 32 (over z, x).
Axes of the slice: x: 4, y: 4 (y_hi: 2, y_lo: 2; y = y_hi * 2 + y_lo), z: 8, core: 2. Of those that a mesh axis runs over, the one named last changes fastest.
Arguments:
- teacher_heads: bfloat16 [512, 8192], P(('group', 'seq'), 'tensor'), may hold values from -6 to 6
- teacher_out: bfloat16 [8192, 16384], P('tensor', 'seq'), may hold values from -0.0625 to 0.0625
- teacher_resid: bfloat16 [512, 16384], P('group', ('seq', 'tensor')), may hold values from -6 to 6
- matches: int32 [1024], P('group'), may hold values from 0 to 127
- projector: bfloat16 [16384, 8192], P(('seq', 'tensor')), may hold values from -0.046875 to 0.046875
- student_heads: bfloat16 [1024, 4096], P(('group', 'seq'), 'tensor'), may hold values from -6 to 6
- student_out: bfloat16 [4096, 8192], P('tensor'), may hold values from -0.09375 to 0.09375
- student_resid: bfloat16 [1024, 8192], P(('group', 'seq', 'tensor')), may hold values from -36 to 36
Outputs:
- loss: float32 [1], replicated
- grad_heads: bfloat16 [1024, 4096], P(('group', 'seq'), 'tensor')
- grad_weight: bfloat16 [4096, 8192], P('tensor', ('group', 'seq'))
The draws below stay inside these ranges and needn't reach their ends.
Inputs may be any that keep to these rules, and one draw needn't show every extreme that they name: `matches`: each student row names a teacher row of its own window by its index within that window.
All inputs are finite; a program needn't handle non-finite values.
Results may differ from the reference program's by a relative error of at most 0.023.
Values may be sent and summed in bfloat16 or wider, within the bound.
No kernel may reach another device: no remote copies, remote signals or barrier semaphores. Data moves between devices by JAX's collectives and lax.ppermute only.
A program may use at most 128 MiB of HBM per device.

```python
import jax
import jax.numpy as jnp
from jax import lax

DT = 16384
HT = 8192
DS = 8192
HS = 4096
T_WIN = 128
S_WIN = 256
WINDOWS = 4
N_TENSOR = 32


def draw_student_resid(key, part):
    key = jax.random.fold_in(key, 7)
    total = WINDOWS * S_WIN
    ramp = jnp.arange(total, dtype=jnp.float32)[:, None] / (total - 1)
    base = jnp.clip(jax.random.normal(key, (total, DS), jnp.float32), -4.0, 4.0)
    scale = 3.0 ** ramp
    return (base * scale).astype(jnp.bfloat16)


def set_ends(values, key, low, top_value):
    shape = values.shape
    spot = [jax.random.randint(jax.random.fold_in(key, axis), (), 0, shape[axis]) for axis in range(len(shape))]
    values = values.at[tuple(spot)].set(low)
    longest = shape.index(max(shape))
    spot[longest] = (spot[longest] + 1) % shape[longest]
    return values.at[tuple(spot)].set(top_value)


def block_scale(own_key, extent, cuts, low, high):
    loudness = 1.0
    for axis_at, blocks in cuts:
        draws = jax.random.uniform(jax.random.fold_in(jax.random.fold_in(own_key, 6), axis_at), (blocks,), jnp.float32, low / len(cuts), high / len(cuts))
        loudness = loudness * jnp.repeat(jnp.exp(draws), extent[axis_at] // blocks).reshape((-1,) + (1,) * (len(extent) - 1 - axis_at))
    return loudness


def centred(key, dims, spread, reach, cuts=(), kind=jnp.bfloat16):
    result = jax.random.normal(key, dims, jnp.float32) * spread
    if len(cuts) > 0:
        result = block_scale(key, dims, cuts, -0.22, 0.18) * result
    return jnp.clip(result, min=-reach, max=reach).astype(kind)


def setup_inputs(seed: int = 0) -> dict:
    arg_keys = jax.random.split(jax.random.key(seed), 9)
    teacher_heads = centred(arg_keys[0], (WINDOWS * T_WIN, HT), 1.0, 6.0, ((0, 8), (1, 32)))
    teacher_out = centred(arg_keys[1], (HT, DT), HT ** -0.5, 0.0625, ((0, 32), (1, 2)))
    teacher_resid = centred(arg_keys[2], (WINDOWS * T_WIN, DT), 1.0, 6.0, ((0, 4), (1, 64)))
    matches = set_ends(jax.random.randint(arg_keys[3], (WINDOWS * S_WIN,), 0, T_WIN), jax.random.fold_in(arg_keys[3], 1), 0, T_WIN - 1).astype(jnp.int32)
    projector = centred(arg_keys[4], (DT, DS), DT ** -0.5, 0.046875, ((0, 64),))
    student_heads = centred(arg_keys[5], (WINDOWS * S_WIN, HS), 1.0, 6.0, ((0, 8), (1, 32)))
    student_out = centred(arg_keys[6], (HS, DS), HS ** -0.5, 0.09375, ((0, 32),))
    student_resid = draw_student_resid(jax.random.fold_in(arg_keys[8], 71), 0)
    return {"teacher_heads": teacher_heads, "teacher_out": teacher_out, "teacher_resid": teacher_resid, "matches": matches, "projector": projector, "student_heads": student_heads, "student_out": student_out, "student_resid": student_resid}


def block_sum(left, right, groups):
    width = left.shape[1] // groups

    def add_block(index, total):
        first = (index * width).astype(jnp.int32)
        left_block = lax.dynamic_slice_in_dim(left, first, width, 1).astype(jnp.float32)
        right_block = lax.dynamic_slice_in_dim(right, first, width, 0).astype(jnp.float32)
        term = jnp.dot(left_block, right_block, preferred_element_type=jnp.float32)
        rounded = lax.optimization_barrier(term.astype(jnp.bfloat16))
        return total + rounded.astype(jnp.float32)

    empty = jnp.zeros((left.shape[0], right.shape[1]), jnp.float32)
    return lax.fori_loop(0, groups, add_block, empty)


def reference(teacher_heads, teacher_out, teacher_resid, matches, projector, student_heads, student_out, student_resid):
    teacher_sum = block_sum(teacher_heads, teacher_out, N_TENSOR)
    teacher_hidden = (teacher_resid.astype(jnp.float32) + teacher_sum).astype(jnp.bfloat16)
    window = jnp.arange(WINDOWS * S_WIN, dtype=jnp.int32) // S_WIN
    rows = (window * T_WIN + matches).astype(jnp.int32)
    selected = jnp.take(teacher_hidden, rows, axis=0)
    projected = jnp.dot(selected, projector, preferred_element_type=jnp.float32)
    student_sum = block_sum(student_heads, student_out, N_TENSOR)
    difference = student_resid.astype(jnp.float32) + student_sum - projected
    loss = jnp.mean(difference * difference).reshape(1)
    grad_hidden = (difference * 0.125).astype(jnp.bfloat16)
    grad_heads = jnp.dot(grad_hidden, student_out.T, preferred_element_type=jnp.float32).astype(jnp.bfloat16)
    grad_weight = jnp.dot(student_heads.T, grad_hidden, preferred_element_type=jnp.float32).astype(jnp.bfloat16)
    return loss, grad_heads, grad_weight
```

```python
import jax
import jax.numpy as jnp
from jax import lax
from jax.sharding import Mesh, PartitionSpec as P

B16 = jnp.bfloat16
F32 = jnp.float32
NY, NZ, NX = 8, 8, 4
GROUP = ("ylo", "core")
COLUMN = ("ylo", "core", "seq")
PLANE = ("z", "x")
ROWS = 1024
COLS = 1024


def dot(a, b, dims):
    return lax.dot_general(a, b, (dims, ((), ())), preferred_element_type=F32)


def spread(block, axis, parts):
    return lax.all_to_all(jnp.broadcast_to(block[None], (parts,) + block.shape), axis, 0, 0)


def scatter_sum(parts):
    over_x = lax.all_to_all(parts, "x", 0, 0)
    summed = jnp.sum(over_x.astype(F32), axis=0).astype(B16)
    over_z = lax.all_to_all(summed, "z", 0, 0)
    return jnp.sum(over_z.astype(F32), axis=0)


def own_order(rows):
    rest = rows.shape[2:]
    parts = rows.reshape((NY, NZ, NX, 4) + rest)
    return jnp.transpose(parts, (2, 1, 0, 3) + tuple(range(4, parts.ndim))).reshape((ROWS,) + rest)


def block_order(rows):
    rest = rows.shape[1:]
    parts = rows.reshape((NX, NZ, NY, 4) + rest)
    return jnp.transpose(parts, (2, 1, 0, 3) + tuple(range(4, parts.ndim))).reshape((NY, 128) + rest)


def local(
    teacher_heads,
    teacher_out,
    teacher_resid,
    matches,
    projector,
    student_heads,
    student_out,
    student_resid,
):
    seq = lax.axis_index("seq")
    member = lax.axis_index(COLUMN)

    away = lax.dynamic_slice(projector, (0, (member + 1 - 2 * seq) * COLS), (256, COLS))
    home = lax.dynamic_slice(projector, (0, member * COLS), (256, COLS))
    other = lax.ppermute(away, "seq", [(0, 1), (1, 0)])
    first = jnp.where(seq == 0, home, other)
    second = jnp.where(seq == 0, other, home)
    out_cols = lax.dynamic_slice(student_out, (0, member * COLS), (128, COLS))

    own_matches = lax.dynamic_slice(matches, (seq * 128,), (128,)).astype(B16)
    shared = jnp.concatenate(
        [
            student_heads,
            teacher_heads[:, :128],
            teacher_heads[:, 128:],
            jnp.broadcast_to(own_matches[None], (16, 128)),
        ],
        axis=0,
    )
    resid_parts = jnp.transpose(student_resid.reshape(4, NY, 8, 128), (1, 0, 2, 3)).reshape(NY, 32, 128)
    sent = jnp.concatenate(
        [jnp.broadcast_to(shared[None], (NY,) + shared.shape), resid_parts], axis=1
    )
    got = lax.all_to_all(sent, COLUMN, 0, 0)
    heads = own_order(got[:, :128])
    pair = lax.dynamic_slice(got, (member - seq, 128, 0), (2, 128, 128))
    window = jnp.concatenate([pair[:, :64], pair[:, 64:]], axis=2).reshape(128, 256)
    base = (jnp.arange(NY, dtype=jnp.int32) // 2 * 128)[:, None]
    picked = own_order(got[:, 256].astype(jnp.int32) + base)
    resid = got[:, 272:].reshape(32, COLS)

    product = dot(window, teacher_out, ((1,), (0,))).astype(B16)
    parts = jnp.transpose(product.reshape(128, NZ, NX, 256), (2, 1, 0, 3))
    hidden = (teacher_resid.astype(F32) + scatter_sum(parts)).astype(B16)

    every = spread(hidden, COLUMN, NY).reshape(4, 2, 128, 256)
    low = every[:, 0].reshape(512, 256)
    high = every[:, 1].reshape(512, 256)
    choose = (picked[:, None] == jnp.arange(512, dtype=jnp.int32)[None]).astype(B16)
    low = dot(choose, low, ((1,), (0,))).astype(B16)
    high = dot(choose, high, ((1,), (0,))).astype(B16)
    partial = (
        dot(heads, out_cols, ((1,), (0,)))
        - dot(low, first, ((1,), (0,)))
        - dot(high, second, ((1,), (0,)))
    ).astype(B16)
    difference = resid.astype(F32) + scatter_sum(partial.reshape(NX, NZ, 32, COLS))
    grad = (difference * 0.125).astype(B16)

    tall = spread(grad, "z", NZ).reshape(256, COLS)
    grad_all = lax.all_gather(tall, "x", axis=0, tiled=True)

    grad_weight = dot(heads, grad_all, ((0,), (0,))).astype(B16)
    heads_part = block_order(dot(grad_all, out_cols, ((1,), (1,))).astype(B16))
    wide = grad_all.astype(F32)
    squares = jnp.sum(wide * wide)
    top = lax.reduce_precision(squares, 8, 7)
    middle = lax.reduce_precision(squares - top, 8, 7)
    bottom = squares - top - middle
    scalars = jnp.stack([top, middle, bottom]).astype(B16)
    extra = jnp.broadcast_to(jnp.pad(scalars, (0, 125))[None, None], (NY, 16, 128))
    back = lax.all_to_all(jnp.concatenate([heads_part, extra], axis=1), COLUMN, 0, 0).astype(F32)
    grad_heads = jnp.sum(back[:, :128], axis=0).astype(B16)
    total = jnp.sum(back[:, 128, :3])
    loss = (total * (64.0 / (ROWS * 8192))).reshape(1)
    return (loss, grad_heads, grad_weight)


def solution(mesh):
    cut = Mesh(mesh.devices.reshape(2, 2, 2, NZ, NX), COLUMN + PLANE)
    every = COLUMN + PLANE
    return jax.shard_map(
        local,
        mesh=cut,
        in_specs=(
            P(COLUMN, PLANE),
            P(PLANE, "seq"),
            P(GROUP, ("seq",) + PLANE),
            P(GROUP),
            P(("seq",) + PLANE, None),
            P(COLUMN, PLANE),
            P(PLANE, None),
            P(every, None),
        ),
        out_specs=(P(), P(COLUMN, PLANE), P(PLANE, COLUMN)),
        check_vma=False,
    )
```

```python
import jax
import jax.numpy as jnp
from jax import lax
from jax.experimental import pallas as pl
from jax.experimental.pallas import tpu as pltpu
from jax.sharding import Mesh, PartitionSpec as P

B16 = jnp.bfloat16
F32 = jnp.float32
NY, NZ, NX = 8, 8, 4
GROUP = ("ylo", "core")
COLUMN = ("ylo", "core", "seq")
PLANE = ("z", "x")
ROWS = 1024
COLS = 1024
PARAMS = pltpu.CompilerParams(vmem_limit_bytes=40 * 1024 * 1024)


def dot(a, b, dims):
    return lax.dot_general(a, b, (dims, ((), ())), preferred_element_type=F32)


def spread(block, axis, parts):
    return lax.all_to_all(jnp.broadcast_to(block[None], (parts,) + block.shape), axis, 0, 0)


def scatter_sum(parts):
    over_x = lax.all_to_all(parts, "x", 0, 0)
    summed = jnp.sum(over_x.astype(F32), axis=0).astype(B16)
    over_z = lax.all_to_all(summed, "z", 0, 0)
    return jnp.sum(over_z.astype(F32), axis=0)


def own_order(rows):
    rest = rows.shape[2:]
    parts = rows.reshape((NY, NZ, NX, 4) + rest)
    return jnp.transpose(parts, (2, 1, 0, 3) + tuple(range(4, parts.ndim))).reshape((ROWS,) + rest)


def block_order(rows):
    rest = rows.shape[1:]
    parts = rows.reshape((NX, NZ, NY, 4) + rest)
    return jnp.transpose(parts, (2, 1, 0, 3) + tuple(range(4, parts.ndim))).reshape((NY, 128) + rest)


def teacher_kernel(heads_ref, out_ref, parts_ref):
    product = dot(heads_ref[...], out_ref[...], ((1,), (0,))).astype(B16)
    for x in range(NX):
        parts_ref[x, 0] = product[:, x * 256 : (x + 1) * 256]


def teacher_parts(window, teacher_out):
    return pl.pallas_call(
        teacher_kernel,
        grid=(NZ,),
        in_specs=[
            pl.BlockSpec((128, 256), lambda i: (0, 0)),
            pl.BlockSpec((256, 1024), lambda i: (0, i)),
        ],
        out_specs=pl.BlockSpec((NX, 1, 128, 256), lambda i: (0, i, 0, 0)),
        out_shape=jax.ShapeDtypeStruct((NX, NZ, 128, 256), B16),
        compiler_params=PARAMS,
        cost_estimate=pl.CostEstimate(flops=2 * 128 * 256 * 8192, bytes_accessed=6 << 20, transcendentals=0),
    )(window, teacher_out)


def combine_kernel(place_ref, picked_ref, got_ref, heads_ref, out_ref, home_ref, other_ref, parts_ref, hidden_ref):
    seq = place_ref[1]

    @pl.when(pl.program_id(0) == 0)
    def _():
        for g in range(4):
            rows = slice(g * 128, (g + 1) * 128)
            hidden_ref[rows, 0:128] = got_ref[2 * g + seq, 0:128, :]
            hidden_ref[rows, 128:256] = got_ref[2 * g + seq, 128:256, :]
            hidden_ref[rows, 256:384] = got_ref[2 * g + 1 - seq, 0:128, :]
            hidden_ref[rows, 384:512] = got_ref[2 * g + 1 - seq, 128:256, :]

    row = lax.broadcasted_iota(jnp.int32, (512, 256), 0)
    choose = (row == picked_ref[0]).astype(F32).astype(B16)
    selected = dot(choose, hidden_ref[...], ((0,), (0,))).astype(B16)
    total = dot(heads_ref[...], out_ref[...], ((1,), (0,)))
    total -= dot(selected[:, :256], home_ref[...], ((1,), (0,)))
    total -= dot(selected[:, 256:], other_ref[...], ((1,), (0,)))
    parts_ref[...] = total.astype(B16)


def combined_parts(place, picked, got, heads, student_out, projector, other):
    return pl.pallas_call(
        combine_kernel,
        grid_spec=pltpu.PrefetchScalarGridSpec(
            num_scalar_prefetch=1,
            grid=(NX,),
            in_specs=[
                pl.BlockSpec((1, 1, 256), lambda i, m: (i, 0, 0)),
                pl.BlockSpec(got.shape, lambda i, m: (0, 0, 0)),
                pl.BlockSpec((256, 128), lambda i, m: (i, 0)),
                pl.BlockSpec((128, COLS), lambda i, m: (0, m[0])),
                pl.BlockSpec((256, COLS), lambda i, m: (0, m[0])),
                pl.BlockSpec((256, COLS), lambda i, m: (0, 0)),
            ],
            out_specs=pl.BlockSpec((256, COLS), lambda i, m: (i, 0)),
            scratch_shapes=[pltpu.VMEM((512, 512), B16)],
        ),
        out_shape=jax.ShapeDtypeStruct((ROWS, COLS), B16),
        compiler_params=PARAMS,
        cost_estimate=pl.CostEstimate(flops=2 * 1024 * 1024 * 900, bytes_accessed=5 << 20, transcendentals=0),
    )(place, picked, got, heads, student_out, projector, other)


def heads_kernel(place_ref, grad_ref, out_ref, part_ref, squares_ref):
    grad = grad_ref[...]
    part_ref[...] = dot(grad, out_ref[...], ((1,), (1,))).astype(B16)
    wide = grad.astype(F32)
    squares = jnp.sum(wide * wide)

    @pl.when(pl.program_id(0) == 0)
    def _():
        squares_ref[0, 0] = squares

    @pl.when(pl.program_id(0) > 0)
    def _():
        squares_ref[0, 0] += squares


def heads_parts(place, grad_all, student_out):
    return pl.pallas_call(
        heads_kernel,
        grid_spec=pltpu.PrefetchScalarGridSpec(
            num_scalar_prefetch=1,
            grid=(NX,),
            in_specs=[
                pl.BlockSpec((256, COLS), lambda i, m: (i, 0)),
                pl.BlockSpec((128, COLS), lambda i, m: (0, m[0])),
            ],
            out_specs=[
                pl.BlockSpec((256, 128), lambda i, m: (i, 0)),
                pl.BlockSpec(memory_space=pltpu.SMEM),
            ],
        ),
        out_shape=[
            jax.ShapeDtypeStruct((ROWS, 128), B16),
            jax.ShapeDtypeStruct((1, 1), F32),
        ],
        compiler_params=PARAMS,
        cost_estimate=pl.CostEstimate(flops=2 * 1024 * 1024 * 128, bytes_accessed=3 << 20, transcendentals=0),
    )(place, grad_all, student_out)


def local(
    teacher_heads,
    teacher_out,
    teacher_resid,
    matches,
    projector,
    student_heads,
    student_out,
    student_resid,
):
    seq = lax.axis_index("seq")
    member = lax.axis_index(COLUMN)
    place = jnp.stack([member, seq]).astype(jnp.int32)
    swap = [(0, 1), (1, 0)]

    there = lax.ppermute(teacher_heads, "seq", swap)
    window = jnp.where(
        seq == 0,
        jnp.concatenate([teacher_heads, there], axis=0),
        jnp.concatenate([there, teacher_heads], axis=0),
    )
    parts = teacher_parts(window, teacher_out)
    hidden = (teacher_resid.astype(F32) + scatter_sum(parts)).astype(B16)

    away = lax.dynamic_slice(projector, (0, (member + 1 - 2 * seq) * COLS), (256, COLS))
    other = lax.ppermute(away, "seq", swap)

    own_matches = lax.dynamic_slice(matches, (seq * 128,), (128,)).astype(B16)
    shared = jnp.concatenate(
        [hidden[:, :128], hidden[:, 128:], student_heads, jnp.broadcast_to(own_matches[None], (16, 128))],
        axis=0,
    )
    resid_parts = jnp.transpose(student_resid.reshape(4, NY, 8, 128), (1, 0, 2, 3)).reshape(NY, 32, 128)
    sent = jnp.concatenate(
        [jnp.broadcast_to(shared[None], (NY,) + shared.shape), resid_parts], axis=1
    )
    got = lax.all_to_all(sent, COLUMN, 0, 0)
    heads = own_order(got[:, 256:384])
    base = (jnp.arange(NY, dtype=jnp.int32) // 2 * 128)[:, None]
    picked = own_order(got[:, 384].astype(jnp.int32) + base).reshape(NX, 1, 256)
    resid = got[:, 400:].reshape(32, COLS)

    partial = combined_parts(place, picked, got, heads, student_out, projector, other)
    difference = resid.astype(F32) + scatter_sum(partial.reshape(NX, NZ, 32, COLS))
    grad = (difference * 0.125).astype(B16)

    tall = spread(grad, "z", NZ).reshape(256, COLS)
    grad_all = spread(tall, "x", NX).reshape(ROWS, COLS)

    heads_part, squares = heads_parts(place, grad_all, student_out)
    squares = squares[0, 0]
    top = lax.reduce_precision(squares, 8, 7)
    middle = lax.reduce_precision(squares - top, 8, 7)
    bottom = squares - top - middle
    scalars = jnp.stack([top, middle, bottom]).astype(B16)
    extra = jnp.broadcast_to(jnp.pad(scalars, (0, 125))[None, None], (NY, 16, 128))
    back = lax.all_to_all(
        jnp.concatenate([block_order(heads_part), extra], axis=1), COLUMN, 0, 0
    ).astype(F32)
    grad_weight = dot(heads, grad_all, ((0,), (0,))).astype(B16)
    grad_heads = jnp.sum(back[:, :128], axis=0).astype(B16)
    total = jnp.sum(back[:, 128, :3])
    loss = (total * (64.0 / (ROWS * 8192))).reshape(1)
    return (loss, grad_heads, grad_weight)


def solution(mesh):
    cut = Mesh(mesh.devices.reshape(2, 2, 2, NZ, NX), COLUMN + PLANE)
    every = COLUMN + PLANE
    return jax.shard_map(
        local,
        mesh=cut,
        in_specs=(
            P(COLUMN, PLANE),
            P(PLANE, "seq"),
            P(GROUP, ("seq",) + PLANE),
            P(GROUP),
            P(("seq",) + PLANE, None),
            P(COLUMN, PLANE),
            P(PLANE, None),
            P(every, None),
        ),
        out_specs=(P(), P(COLUMN, PLANE), P(PLANE, COLUMN)),
        check_vma=False,
    )
```

```python
import jax
import jax.numpy as jnp
from jax import lax
from jax.experimental import pallas as pl
from jax.experimental.pallas import tpu as pltpu
from jax.sharding import Mesh, PartitionSpec as P

B16 = jnp.bfloat16
F32 = jnp.float32
NY, NZ, NX = 8, 8, 4
GROUP = ("ylo", "core")
COLUMN = ("ylo", "core", "seq")
PLANE = ("z", "x")
ROWS = 1024
COLS = 1024
HALF = COLS // 2
PARAMS = pltpu.CompilerParams(vmem_limit_bytes=56 * 1024 * 1024)


def dot(a, b, dims):
    return lax.dot_general(a, b, (dims, ((), ())), preferred_element_type=F32)


def add(a, b):
    return (a.astype(F32) + b.astype(F32)).astype(B16)


def across(block, flip):
    return lax.ppermute(block, "x", [(i, i ^ flip) for i in range(NX)])


def reduce_x(first, second):
    from_one = across(first[1:3], 1)
    from_three = across(second[2:4], 3)
    mine = first[0].astype(F32) + from_one[0].astype(F32)
    pass_on = add(first[3], from_one[1])
    last_three = across(pass_on, 3)
    theirs = second[0].astype(F32) + from_three[1].astype(F32)
    pass_back = add(second[1], from_three[0])
    last_one = across(pass_back, 1)
    return (
        (mine + last_three.astype(F32)).astype(B16),
        (theirs + last_one.astype(F32)).astype(B16),
    )


def gather_x(first, second):
    pair = jnp.stack([first, across(first, 3)])
    other = jnp.stack([second, across(second, 1)])
    return pair, across(pair, 1), other, across(other, 3)


def reduce_z(parts):
    moved = lax.all_to_all(parts, "z", 0, 0)
    return jnp.sum(moved.astype(F32), axis=0)


def own_order(rows):
    rest = rows.shape[2:]
    parts = rows.reshape((NY, NZ, NX, 4) + rest)
    return jnp.transpose(parts, (2, 1, 0, 3) + tuple(range(4, parts.ndim))).reshape((ROWS,) + rest)


def block_order(rows):
    rest = rows.shape[1:]
    parts = rows.reshape((NX, NZ, NY, 4) + rest)
    return jnp.transpose(parts, (2, 1, 0, 3) + tuple(range(4, parts.ndim))).reshape((NY, 128) + rest)


def teacher_kernel(place_ref, own_ref, there_ref, out_ref, first_ref, second_ref, window_ref):
    seq, x = place_ref[1], place_ref[2]

    @pl.when(pl.program_id(0) == 0)
    def _():
        window_ref[pl.ds(pl.multiple_of(seq * 64, 64), 64), :] = own_ref[...]
        window_ref[pl.ds(pl.multiple_of(64 - seq * 64, 64), 64), :] = there_ref[...]

    product = dot(window_ref[...], out_ref[...], ((1,), (0,))).astype(B16)
    for to in range(NX):
        first_ref[to ^ x, 0] = product[:, to * 256 : to * 256 + 128]
        second_ref[to ^ x, 0] = product[:, to * 256 + 128 : to * 256 + 256]


def teacher_parts(place, own, there, teacher_out):
    half = pl.BlockSpec((NX, 1, 128, 128), lambda i, m: (0, i, 0, 0))
    return pl.pallas_call(
        teacher_kernel,
        grid_spec=pltpu.PrefetchScalarGridSpec(
            num_scalar_prefetch=1,
            grid=(NZ,),
            in_specs=[
                pl.BlockSpec((64, 256), lambda i, m: (0, 0)),
                pl.BlockSpec((64, 256), lambda i, m: (0, 0)),
                pl.BlockSpec((256, 1024), lambda i, m: (0, i)),
            ],
            out_specs=[half, half],
            scratch_shapes=[pltpu.VMEM((128, 256), B16)],
        ),
        out_shape=[jax.ShapeDtypeStruct((NX, NZ, 128, 128), B16)] * 2,
        compiler_params=PARAMS,
        cost_estimate=pl.CostEstimate(flops=2 * 128 * 256 * 8192, bytes_accessed=6 << 20, transcendentals=0),
    )(place, own, there, teacher_out)


def combine_kernel(
    place_ref, picked_ref, got_ref, heads_ref, out_ref, home_ref, other_ref, first_ref, second_ref, hidden_ref
):
    seq = place_ref[1]

    @pl.when(pl.program_id(0) == 0)
    def _():
        for g in range(4):
            rows = slice(g * 128, (g + 1) * 128)
            hidden_ref[rows, 0:128] = got_ref[2 * g + seq, 0:128, :]
            hidden_ref[rows, 128:256] = got_ref[2 * g + seq, 128:256, :]
            hidden_ref[rows, 256:384] = got_ref[2 * g + 1 - seq, 0:128, :]
            hidden_ref[rows, 384:512] = got_ref[2 * g + 1 - seq, 128:256, :]

    row = lax.broadcasted_iota(jnp.int32, (512, 256), 0)
    choose = (row == picked_ref[0]).astype(F32).astype(B16)
    selected = dot(choose, hidden_ref[...], ((0,), (0,))).astype(B16)
    total = dot(heads_ref[...], out_ref[...], ((1,), (0,)))
    total -= dot(selected[:, :256], home_ref[...], ((1,), (0,)))
    total -= dot(selected[:, 256:], other_ref[...], ((1,), (0,)))
    first_ref[0] = total[:, :HALF].astype(B16)
    second_ref[0] = total[:, HALF:].astype(B16)


def combined_parts(place, picked, got, heads, student_out, projector, other):
    half = pl.BlockSpec((1, 256, HALF), lambda i, m: (i, 0, 0))
    return pl.pallas_call(
        combine_kernel,
        grid_spec=pltpu.PrefetchScalarGridSpec(
            num_scalar_prefetch=1,
            grid=(NX,),
            in_specs=[
                pl.BlockSpec((1, 1, 256), lambda i, m: (i ^ m[2], 0, 0)),
                pl.BlockSpec(got.shape, lambda i, m: (0, 0, 0)),
                pl.BlockSpec((256, 128), lambda i, m: (i ^ m[2], 0)),
                pl.BlockSpec((128, COLS), lambda i, m: (0, m[0])),
                pl.BlockSpec((256, COLS), lambda i, m: (0, m[0])),
                pl.BlockSpec((256, COLS), lambda i, m: (0, 0)),
            ],
            out_specs=[half, half],
            scratch_shapes=[pltpu.VMEM((512, 512), B16)],
        ),
        out_shape=[jax.ShapeDtypeStruct((NX, 256, HALF), B16)] * 2,
        compiler_params=PARAMS,
        cost_estimate=pl.CostEstimate(flops=2 * 1024 * 1024 * 900, bytes_accessed=5 << 20, transcendentals=0),
    )(place, picked, got, heads, student_out, projector, other)


def gradient_parts(pair_ref, far_ref, other_ref, off_ref):
    return (
        (0, pair_ref[0], other_ref[0]),
        (1, far_ref[0], other_ref[1]),
        (2, far_ref[1], off_ref[1]),
        (3, pair_ref[1], off_ref[0]),
    )


def heads_kernel(place_ref, pair_ref, far_ref, other_ref, off_ref, out_ref, part_ref, squares_ref, sums_ref):
    x = place_ref[2]
    for k, first, second in gradient_parts(pair_ref, far_ref, other_ref, off_ref):
        part = dot(first, out_ref[:, :HALF], ((1,), (1,))) + dot(second, out_ref[:, HALF:], ((1,), (1,)))
        part_ref[k ^ x] = part.astype(B16)
        wide = first.astype(F32)
        more = second.astype(F32)
        line = jnp.sum(wide * wide + more * more, axis=0, keepdims=True)
        sums_ref[k ^ x] = line[:, :128] + line[:, 128:256] + line[:, 256:384] + line[:, 384:]
    total = sums_ref[0] + sums_ref[1] + sums_ref[2] + sums_ref[3]
    top = total.astype(B16).astype(F32)
    middle = (total - top).astype(B16).astype(F32)
    bottom = total - top - middle
    row = lax.broadcasted_iota(jnp.int32, (16, 128), 0)
    lines = jnp.where(row == 0, top, jnp.where(row == 1, middle, jnp.where(row == 2, bottom, 0.0)))
    squares_ref[...] = lines.astype(B16)


def weight_kernel(place_ref, pair_ref, far_ref, other_ref, off_ref, heads_ref, weight_ref):
    x = place_ref[2]
    left = jnp.zeros((128, HALF), F32)
    right = jnp.zeros((128, HALF), F32)
    for k, first, second in gradient_parts(pair_ref, far_ref, other_ref, off_ref):
        heads = heads_ref[k ^ x]
        left += dot(heads, first, ((0,), (0,)))
        right += dot(heads, second, ((0,), (0,)))
    weight_ref[:, :HALF] = left.astype(B16)
    weight_ref[:, HALF:] = right.astype(B16)


QUARTERS = pl.BlockSpec((2, 256, HALF), lambda i, m: (0, 0, 0))


def heads_parts(place, gathered, student_out):
    return pl.pallas_call(
        heads_kernel,
        grid_spec=pltpu.PrefetchScalarGridSpec(
            num_scalar_prefetch=1,
            grid=(1,),
            in_specs=[QUARTERS] * 4 + [pl.BlockSpec((128, COLS), lambda i, m: (0, m[0]))],
            out_specs=[
                pl.BlockSpec((NX, 256, 128), lambda i, m: (0, 0, 0)),
                pl.BlockSpec((16, 128), lambda i, m: (0, 0)),
            ],
            scratch_shapes=[pltpu.VMEM((NX, 1, 128), F32)],
        ),
        out_shape=[
            jax.ShapeDtypeStruct((NX, 256, 128), B16),
            jax.ShapeDtypeStruct((16, 128), B16),
        ],
        compiler_params=pltpu.CompilerParams(vmem_limit_bytes=24 * 1024 * 1024),
        cost_estimate=pl.CostEstimate(flops=2 * 1024 * 1024 * 128, bytes_accessed=3 << 20, transcendentals=0),
    )(place, *gathered, student_out)


def weight_grad(place, gathered, heads):
    return pl.pallas_call(
        weight_kernel,
        grid_spec=pltpu.PrefetchScalarGridSpec(
            num_scalar_prefetch=1,
            grid=(1,),
            in_specs=[QUARTERS] * 4 + [pl.BlockSpec((NX, 256, 128), lambda i, m: (0, 0, 0))],
            out_specs=pl.BlockSpec((128, COLS), lambda i, m: (0, 0)),
        ),
        out_shape=jax.ShapeDtypeStruct((128, COLS), B16),
        compiler_params=pltpu.CompilerParams(vmem_limit_bytes=24 * 1024 * 1024),
        cost_estimate=pl.CostEstimate(flops=2 * 1024 * 1024 * 128, bytes_accessed=3 << 20, transcendentals=0),
    )(place, *gathered, heads)


def local(
    teacher_heads,
    teacher_out,
    teacher_resid,
    matches,
    projector,
    student_heads,
    student_out,
    student_resid,
):
    seq = lax.axis_index("seq")
    member = lax.axis_index(COLUMN)
    place = jnp.stack([member, seq, lax.axis_index("x")]).astype(jnp.int32)
    swap = [(0, 1), (1, 0)]

    there = lax.ppermute(teacher_heads, "seq", swap)
    first, second = reduce_x(*teacher_parts(place, teacher_heads, there, teacher_out))
    halves = jnp.concatenate([first, second], axis=1)

    away = lax.dynamic_slice(projector, (0, (member + 1 - 2 * seq) * COLS), (256, COLS))
    other = lax.ppermute(away, "seq", swap)
    halves, other = lax.optimization_barrier((halves, other))
    resid_halves = jnp.concatenate([teacher_resid[:, :128], teacher_resid[:, 128:]], axis=0)
    hidden = (resid_halves.astype(F32) + reduce_z(halves)).astype(B16)

    own_matches = lax.dynamic_slice(matches, (seq * 128,), (128,)).astype(B16)
    shared = jnp.concatenate(
        [hidden, student_heads, jnp.broadcast_to(own_matches[None], (16, 128))], axis=0
    )
    resid_parts = jnp.transpose(student_resid.reshape(4, NY, 8, 128), (1, 0, 2, 3)).reshape(NY, 32, 128)
    sent = jnp.concatenate(
        [jnp.broadcast_to(shared[None], (NY,) + shared.shape), resid_parts], axis=1
    )
    got = lax.all_to_all(sent, COLUMN, 0, 0)
    heads = own_order(got[:, 256:384])
    base = (jnp.arange(NY, dtype=jnp.int32) // 2 * 128)[:, None]
    picked = own_order(got[:, 384].astype(jnp.int32) + base).reshape(NX, 1, 256)
    resid = got[:, 400:].reshape(32, 2, HALF)
    resid = jnp.concatenate([resid[:, 0], resid[:, 1]], axis=0)

    first, second = combined_parts(place, picked, got, heads, student_out, projector, other)
    first, second = reduce_x(
        first.reshape(NX, NZ, 32, HALF), second.reshape(NX, NZ, 32, HALF)
    )
    summed = reduce_z(jnp.concatenate([first, second], axis=1))
    difference = resid.astype(F32) + summed
    grad = (difference * 0.125).astype(B16)

    tall = lax.all_to_all(jnp.broadcast_to(grad[None], (NZ, 64, HALF)), "z", 0, 0)
    gathered = gather_x(tall[:, :32].reshape(256, HALF), tall[:, 32:].reshape(256, HALF))

    heads_part, squares = heads_parts(place, gathered, student_out)
    sent = jnp.concatenate(
        [block_order(heads_part.reshape(ROWS, 128)), jnp.broadcast_to(squares[None], (NY, 16, 128))], axis=1
    )
    back = lax.all_to_all(sent, COLUMN, 0, 0).astype(F32)
    grad_weight = weight_grad(place, gathered, heads.reshape(NX, 256, 128))
    grad_heads = jnp.sum(back[:, :128], axis=0).astype(B16)
    total = jnp.sum(back[:, 128:])
    loss = (total * (64.0 / (ROWS * 8192))).reshape(1)
    return (loss, grad_heads, grad_weight)


def solution(mesh):
    cut = Mesh(mesh.devices.reshape(2, 2, 2, NZ, NX), COLUMN + PLANE)
    every = COLUMN + PLANE
    return jax.shard_map(
        local,
        mesh=cut,
        in_specs=(
            P(COLUMN, PLANE),
            P(PLANE, "seq"),
            P(GROUP, ("seq",) + PLANE),
            P(GROUP),
            P(("seq",) + PLANE, None),
            P(COLUMN, PLANE),
            P(PLANE, None),
            P(every, None),
        ),
        out_specs=(P(), P(COLUMN, PLANE), P(PLANE, COLUMN)),
        check_vma=False,
    )
```

```python
import functools

import jax
import jax.numpy as jnp
from jax import lax
from jax.experimental import pallas as pl
from jax.experimental.pallas import tpu as pltpu
from jax.sharding import Mesh, PartitionSpec as P

B16 = jnp.bfloat16
F32 = jnp.float32
NY, NZ, NX = 8, 8, 4
GROUP = ("ylo", "core")
COLUMN = ("ylo", "core", "seq")
PLANE = ("z", "x")
ROWS = 1024
COLS = 1024
HALF = COLS // 2
PARAMS = pltpu.CompilerParams(vmem_limit_bytes=32 * 1024 * 1024)


def dot(a, b, dims):
    return lax.dot_general(a, b, (dims, ((), ())), preferred_element_type=F32)


def add(*terms):
    total = terms[0].astype(F32)
    for term in terms[1:]:
        total += term.astype(F32)
    return total.astype(B16)


def across(block, flip):
    return lax.ppermute(block, "x", [(i, i ^ flip) for i in range(NX)])


def reduce_x(first, second, tie=()):
    first_far = across(first[2], 1)
    second_far = across(second[2], 3)
    first_near = across(first[1], 1)
    second_near = across(second[3], 3)
    if tie:
        first_far, second_far, *tie = lax.optimization_barrier((first_far, second_far, *tie))
    first_last = across(add(first[3], first_far), 3)
    second_last = across(add(second[1], second_far), 1)
    return (
        add(first[0], first_near, first_last),
        add(second[0], second_near, second_last),
        *tie,
    )


def gather_x(first, second):
    first_three = across(first, 3)
    second_one = across(second, 1)
    first_one = across(first, 1)
    second_three = across(second, 3)
    first_two = across(first_three, 1)
    second_two = across(second_one, 3)
    return first, first_one, first_two, first_three, second, second_one, second_two, second_three


def reduce_z(parts):
    moved = lax.all_to_all(parts, "z", 0, 0)
    return jnp.sum(moved.astype(F32), axis=0)


def own_order(rows):
    rest = rows.shape[2:]
    parts = rows.reshape((NY, NZ, NX, 4) + rest)
    return jnp.transpose(parts, (2, 1, 0, 3) + tuple(range(4, parts.ndim))).reshape((ROWS,) + rest)


def block_order(rows):
    rest = rows.shape[1:]
    parts = rows.reshape((NX, NZ, NY, 4) + rest)
    return jnp.transpose(parts, (2, 1, 0, 3) + tuple(range(4, parts.ndim))).reshape((NY, 128) + rest)


def whole(*shape):
    return pl.BlockSpec(shape, lambda i, m: (0,) * len(shape))


def call(kernel, in_specs, outs, flops, scratch=()):
    return pl.pallas_call(
        kernel,
        grid_spec=pltpu.PrefetchScalarGridSpec(
            num_scalar_prefetch=1,
            grid=(1,),
            in_specs=in_specs,
            out_specs=[whole(*out.shape) for out in outs],
            scratch_shapes=scratch,
        ),
        out_shape=outs,
        compiler_params=PARAMS,
        cost_estimate=pl.CostEstimate(flops=flops, bytes_accessed=5 << 20, transcendentals=0),
    )


def teacher_kernel(place_ref, rows_ref, out_ref, *parts):
    x = place_ref[2]
    rows = rows_ref[...]
    for z in range(NZ):
        for k in range(NX):
            columns = pl.ds(pl.multiple_of(z * 1024 + (k ^ x) * 256, 256), 256)
            parts[k][z] = dot(rows, out_ref[:, columns], ((1,), (0,))).astype(B16)


def teacher_parts(place, rows, teacher_out):
    outs = [jax.ShapeDtypeStruct((NZ, 64, 256), B16)] * NX
    return call(teacher_kernel, [whole(64, 256), whole(256, 8192)], outs, 2 * 64 * 256 * 8192)(
        place, rows, teacher_out
    )


def gather_hidden(place_ref, got_ref, hidden_ref):
    seq = place_ref[1]
    for g in range(4):
        near = pl.ds(pl.multiple_of(g * 128 + seq * 64, 64), 64)
        far = pl.ds(pl.multiple_of(g * 128 + 64 - seq * 64, 64), 64)
        hidden_ref[near, 0:256] = got_ref[2 * g + seq, 0:64, :]
        hidden_ref[far, 0:256] = got_ref[2 * g + seq, 64:128, :]
        hidden_ref[far, 256:512] = got_ref[2 * g + 1 - seq, 0:64, :]
        hidden_ref[near, 256:512] = got_ref[2 * g + 1 - seq, 64:128, :]


def combine_kernel(jobs, place_ref, picked_ref, got_ref, heads_ref, out_ref, home_ref, other_ref, *refs):
    x = place_ref[2]
    parts, hidden_ref = refs[:-1], refs[-1]
    gather_hidden(place_ref, got_ref, hidden_ref)
    row = lax.broadcasted_iota(jnp.int32, (512, 256), 0)
    for k, halves in jobs:
        choose = (row == picked_ref[k ^ x]).astype(F32).astype(B16)
        selected = dot(choose, hidden_ref[...], ((0,), (0,))).astype(B16)
        heads = heads_ref[k ^ x]
        for half, to in halves:
            columns = slice(half * HALF, (half + 1) * HALF)
            total = dot(heads, out_ref[:, columns], ((1,), (0,)))
            total -= dot(selected[:, :256], home_ref[:, columns], ((1,), (0,)))
            total -= dot(selected[:, 256:], other_ref[:, columns], ((1,), (0,)))
            parts[to][...] = total.astype(B16)


SENT = ((2, ((0, 1), (1, 2))), (1, ((0, 0),)), (3, ((1, 3),)))
KEPT = ((3, ((0, 1),)), (1, ((1, 3),)), (0, ((0, 0), (1, 2))))


def combined_parts(jobs, place, picked, got, heads, student_out, projector, other):
    specs = [
        whole(NX, 1, 256),
        whole(NY, 128, 256),
        whole(NX, 256, 128),
        pl.BlockSpec((128, COLS), lambda i, m: (0, m[0])),
        pl.BlockSpec((256, COLS), lambda i, m: (0, m[0])),
        whole(256, COLS),
    ]
    outs = [jax.ShapeDtypeStruct((256, HALF), B16)] * 4
    return call(
        functools.partial(combine_kernel, jobs), specs, outs, 2 * 512 * 1024 * 900, [pltpu.VMEM((512, 512), B16)]
    )(place, picked, got, heads, student_out, projector, other)


def heads_kernel(place_ref, *refs):
    x = place_ref[2]
    first, second = refs[:4], refs[4:8]
    out_ref, part_ref, squares_ref, sums_ref = refs[8:]
    for k in range(NX):
        near, far = first[k][...], second[k][...]
        part = dot(near, out_ref[:, :HALF], ((1,), (1,))) + dot(far, out_ref[:, HALF:], ((1,), (1,)))
        part_ref[k ^ x] = part.astype(B16)
        near, far = near.astype(F32), far.astype(F32)
        line = jnp.sum(near * near + far * far, axis=0, keepdims=True)
        sums_ref[k ^ x] = line[:, :128] + line[:, 128:256] + line[:, 256:384] + line[:, 384:]
    total = sums_ref[0] + sums_ref[1] + sums_ref[2] + sums_ref[3]
    top = total.astype(B16).astype(F32)
    middle = (total - top).astype(B16).astype(F32)
    bottom = total - top - middle
    row = lax.broadcasted_iota(jnp.int32, (16, 128), 0)
    lines = jnp.where(row == 0, top, jnp.where(row == 1, middle, jnp.where(row == 2, bottom, 0.0)))
    squares_ref[...] = lines.astype(B16)


def weight_kernel(place_ref, *refs):
    x = place_ref[2]
    first, second = refs[:4], refs[4:8]
    heads_ref, weight_ref = refs[8:]
    left = jnp.zeros((128, HALF), F32)
    right = jnp.zeros((128, HALF), F32)
    for k in range(NX):
        heads = heads_ref[k ^ x]
        left += dot(heads, first[k][...], ((0,), (0,)))
        right += dot(heads, second[k][...], ((0,), (0,)))
    weight_ref[:, :HALF] = left.astype(B16)
    weight_ref[:, HALF:] = right.astype(B16)


def heads_parts(place, gathered, student_out):
    specs = [whole(256, HALF)] * 8 + [pl.BlockSpec((128, COLS), lambda i, m: (0, m[0]))]
    outs = [jax.ShapeDtypeStruct((NX, 256, 128), B16), jax.ShapeDtypeStruct((16, 128), B16)]
    return call(heads_kernel, specs, outs, 2 * 1024 * 1024 * 128, [pltpu.VMEM((NX, 1, 128), F32)])(
        place, *gathered, student_out
    )


def weight_grad(place, gathered, heads):
    specs = [whole(256, HALF)] * 8 + [whole(NX, 256, 128)]
    outs = [jax.ShapeDtypeStruct((128, COLS), B16)]
    return call(weight_kernel, specs, outs, 2 * 1024 * 1024 * 128)(place, *gathered, heads)[0]


def local(
    teacher_heads,
    teacher_out,
    teacher_resid,
    matches,
    projector,
    student_heads,
    student_out,
    student_resid,
):
    seq = lax.axis_index("seq")
    member = lax.axis_index(COLUMN)
    place = jnp.stack([member, seq, lax.axis_index("x")]).astype(jnp.int32)
    swap = [(0, 1), (1, 0)]

    away = lax.dynamic_slice(projector, (0, (member + 1 - 2 * seq) * COLS), (256, COLS))
    other = lax.ppermute(away, "seq", swap)

    own_matches = lax.dynamic_slice(matches, (seq * 128,), (128,)).astype(B16)
    shared = jnp.concatenate([student_heads, jnp.broadcast_to(own_matches[None], (16, 128))], axis=0)
    resid_parts = jnp.transpose(student_resid.reshape(4, NY, 8, 128), (1, 0, 2, 3)).reshape(NY, 32, 128)
    early = jnp.concatenate([jnp.broadcast_to(shared[None], (NY,) + shared.shape), resid_parts], axis=1)
    early = lax.all_to_all(early, COLUMN, 0, 0)

    there = lax.ppermute(teacher_heads, "seq", swap)
    first, second, other = reduce_x(
        teacher_parts(place, teacher_heads, teacher_out),
        teacher_parts(place, there, teacher_out),
        (other,),
    )
    summed = jnp.concatenate([first, second], axis=1)
    summed, early = lax.optimization_barrier((summed, early))
    heads = own_order(early[:, :128]).reshape(NX, 256, 128)
    base = (jnp.arange(NY, dtype=jnp.int32) // 2 * 128)[:, None]
    picked = own_order(early[:, 128].astype(jnp.int32) + base).reshape(NX, 1, 256)
    resid = early[:, 144:].reshape(32, 2, HALF)
    resid = jnp.concatenate([resid[:, 0], resid[:, 1]], axis=0)
    near = lax.dynamic_slice(teacher_resid, (seq * 64, 0), (64, 256))
    far = lax.dynamic_slice(teacher_resid, (64 - seq * 64, 0), (64, 256))
    hidden = (jnp.concatenate([near, far], axis=0).astype(F32) + reduce_z(summed)).astype(B16)

    got = lax.all_to_all(jnp.broadcast_to(hidden[None], (NY, 128, 256)), COLUMN, 0, 0)
    operands = (place, picked, got, heads, student_out, projector, other)
    sent = combined_parts(SENT, *operands)
    kept = combined_parts(KEPT, *operands)
    sent = [part.reshape(NZ, 32, HALF) for part in sent]
    kept = [part.reshape(NZ, 32, HALF) for part in kept]
    first, second = reduce_x(
        (kept[0], sent[0], sent[1], kept[1]), (kept[2], kept[3], sent[2], sent[3])
    )
    summed = reduce_z(jnp.concatenate([first, second], axis=1))
    difference = resid.astype(F32) + summed
    grad = (difference * 0.125).astype(B16)

    tall = lax.all_to_all(jnp.broadcast_to(grad[None], (NZ, 64, HALF)), "z", 0, 0)
    gathered = gather_x(tall[:, :32].reshape(256, HALF), tall[:, 32:].reshape(256, HALF))

    heads_part, squares = heads_parts(place, gathered, student_out)
    sent = jnp.concatenate(
        [block_order(heads_part.reshape(ROWS, 128)), jnp.broadcast_to(squares[None], (NY, 16, 128))], axis=1
    )
    back = lax.all_to_all(sent, COLUMN, 0, 0).astype(F32)
    grad_weight = weight_grad(place, gathered, heads)
    grad_heads = jnp.sum(back[:, :128], axis=0).astype(B16)
    total = jnp.sum(back[:, 128:])
    loss = (total * (64.0 / (ROWS * 8192))).reshape(1)
    return (loss, grad_heads, grad_weight)


def solution(mesh):
    cut = Mesh(mesh.devices.reshape(2, 2, 2, NZ, NX), COLUMN + PLANE)
    every = COLUMN + PLANE
    return jax.shard_map(
        local,
        mesh=cut,
        in_specs=(
            P(COLUMN, PLANE),
            P(PLANE, "seq"),
            P(GROUP, ("seq",) + PLANE),
            P(GROUP),
            P(("seq",) + PLANE, None),
            P(COLUMN, PLANE),
            P(PLANE, None),
            P(every, None),
        ),
        out_specs=(P(), P(COLUMN, PLANE), P(PLANE, COLUMN)),
        check_vma=False,
    )
```

```python
import jax
import jax.numpy as jnp
from jax import lax
from jax.experimental import pallas as pl
from jax.experimental.pallas import tpu as pltpu
from jax.sharding import Mesh, PartitionSpec as P

B16 = jnp.bfloat16
F32 = jnp.float32
NY, NZ, NX = 8, 8, 4
GROUP = ("ylo", "core")
COLUMN = ("ylo", "core", "seq")
PLANE = ("z", "x")
ROWS = 1024
COLS = 1024
PARAMS = pltpu.CompilerParams(vmem_limit_bytes=32 * 1024 * 1024)


def dot(a, b, dims):
    return lax.dot_general(a, b, (dims, ((), ())), preferred_element_type=F32)


def add(*terms):
    total = terms[0].astype(F32)
    for term in terms[1:]:
        total += term.astype(F32)
    return total.astype(B16)


def across(block, flip):
    return lax.ppermute(block, "x", [(i, i ^ flip) for i in range(NX)])


def reduce_x(first, second, tie=()):
    first_far = across(first[2], 1)
    second_far = across(second[2], 3)
    first_near = across(first[1], 1)
    second_near = across(second[3], 3)
    if tie:
        first_far, second_far, *tie = lax.optimization_barrier((first_far, second_far, *tie))
    first_last = across(add(first[3], first_far), 3)
    second_last = across(add(second[1], second_far), 1)
    return (
        add(first[0], first_near, first_last),
        add(second[0], second_near, second_last),
        *tie,
    )


def gather_x(first, second):
    first_three = across(first, 3)
    second_one = across(second, 1)
    first_one = across(first, 1)
    second_three = across(second, 3)
    first_two = across(first_three, 1)
    second_two = across(second_one, 3)
    return first, first_one, first_two, first_three, second, second_one, second_two, second_three


def whole(*shape):
    return pl.BlockSpec(shape, lambda i, m: (0,) * len(shape))


def call(kernel, in_specs, outs, flops, scratch=()):
    return pl.pallas_call(
        kernel,
        grid_spec=pltpu.PrefetchScalarGridSpec(
            num_scalar_prefetch=1,
            grid=(1,),
            in_specs=in_specs,
            out_specs=[whole(*out.shape) for out in outs],
            scratch_shapes=scratch,
        ),
        out_shape=outs,
        compiler_params=PARAMS,
        cost_estimate=pl.CostEstimate(flops=flops, bytes_accessed=5 << 20, transcendentals=0),
    )


def teacher_kernel(place_ref, rows_ref, out_ref, *refs):
    x = place_ref[2]
    parts, held, sems = refs[:NX], refs[NX], refs[NX + 1]
    copies = [
        pltpu.make_async_copy(out_ref.at[:, pl.ds(z * 1024, 1024)], held.at[z], sems.at[z]) for z in range(NZ)
    ]
    for copy in copies:
        copy.start()
    rows = rows_ref[...]
    for z in range(NZ):
        copies[z].wait()
        for k in range(NX):
            columns = pl.ds(pl.multiple_of((k ^ x) * 256, 256), 256)
            parts[k][z] = dot(rows, held[z, :, columns], ((1,), (0,))).astype(B16)


def teacher_parts(place, rows, teacher_out):
    outs = [jax.ShapeDtypeStruct((NZ, 64, 256), B16)] * NX
    scratch = [pltpu.VMEM((NZ, 256, 1024), B16), pltpu.SemaphoreType.DMA((NZ,))]
    specs = [whole(64, 256), pl.BlockSpec(memory_space=pl.ANY)]
    return call(teacher_kernel, specs, outs, 2 * 64 * 256 * 8192, scratch)(place, rows, teacher_out)


def student_kernel(place_ref, heads_ref, resid_ref, out_ref, parts_ref):
    plane = place_ref[3]
    row = lax.broadcasted_iota(jnp.int32, (256, 32), 0)
    line = lax.broadcasted_iota(jnp.int32, (256, 32), 1)
    spot = (line // 4) * 128 + plane * 4 + line % 4
    for w in range(NX):
        put = (row + w * 256 == spot).astype(F32).astype(B16)
        heads = jnp.concatenate([heads_ref[2 * w], heads_ref[2 * w + 1]], axis=0)
        total = dot(heads, out_ref[...], ((1,), (0,))) + dot(put, resid_ref[...], ((1,), (0,)))
        total = total.astype(B16)
        for z in range(NZ):
            parts_ref[w, z] = total[:, z * 128 : (z + 1) * 128]


def student_parts(place, heads, resid, out_cols):
    outs = [jax.ShapeDtypeStruct((NX, NZ, 256, 128), B16)]
    specs = [whole(NY, 128, 128), whole(32, COLS), whole(128, COLS)]
    return call(student_kernel, specs, outs, 2 * 1024 * 1024 * 160)(place, heads, resid, out_cols)[0]


def gather_hidden(place_ref, got_ref, hidden_ref):
    seq = place_ref[1]
    for g in range(4):
        near = pl.ds(pl.multiple_of(seq * 64, 64), 64)
        far = pl.ds(pl.multiple_of(64 - seq * 64, 64), 64)
        hidden_ref[g, near, 0:256] = got_ref[2 * g + seq, 0:64, :]
        hidden_ref[g, far, 0:256] = got_ref[2 * g + seq, 64:128, :]
        hidden_ref[g, far, 256:512] = got_ref[2 * g + 1 - seq, 0:64, :]
        hidden_ref[g, near, 256:512] = got_ref[2 * g + 1 - seq, 64:128, :]


def project_kernel(place_ref, got_ref, home_ref, other_ref, *refs):
    x = place_ref[2]
    parts, hidden_ref = refs[:-1], refs[-1]
    gather_hidden(place_ref, got_ref, hidden_ref)
    for k in (2, 1, 3, 0):
        rows = hidden_ref[k ^ x]
        total = dot(rows[:, :256], home_ref[...], ((1,), (0,))) + dot(rows[:, 256:], other_ref[...], ((1,), (0,)))
        total = total.astype(B16)
        for z in range(NZ):
            parts[k][z] = total[:64, z * 128 : (z + 1) * 128]
            parts[NX + k][z] = total[64:, z * 128 : (z + 1) * 128]


def projected_parts(place, got, home, other):
    specs = [whole(NY, 128, 256), whole(256, COLS), whole(256, COLS)]
    outs = [jax.ShapeDtypeStruct((NZ, 64, 128), B16)] * 8
    parts = call(project_kernel, specs, outs, 2 * 512 * 512 * 1024, [pltpu.VMEM((4, 128, 512), B16)])(
        place, got, home, other
    )
    return parts[:NX], parts[NX:]


def gradient_kernel(place_ref, moved_ref, sum_ref, matches_ref, grad_ref):
    projected = moved_ref[0].astype(F32)
    for z in range(1, NZ):
        projected += moved_ref[z].astype(F32)
    high = projected.astype(B16)
    low = (projected - high.astype(F32)).astype(B16)
    row = lax.broadcasted_iota(jnp.int32, (128, 256), 0)
    choose = (row == matches_ref[...]).astype(F32).astype(B16)
    selected = dot(choose, high, ((0,), (0,))) + dot(choose, low, ((0,), (0,)))
    grad = ((sum_ref[...].astype(F32) - selected) * 0.125).astype(B16)
    for z in range(NZ):
        grad_ref[z] = grad


def gradient_piece(place, moved, student_sum, picked):
    specs = [whole(NZ, 128, 128), whole(256, 128), whole(1, 256)]
    outs = [jax.ShapeDtypeStruct((NZ, 256, 128), B16)]
    return call(gradient_kernel, specs, outs, 2 * 256 * 256 * 128)(place, moved, student_sum, picked)[0]


def wide_rows(ref):
    return jnp.concatenate([ref[z] for z in range(NZ)], axis=1)


def heads_kernel(place_ref, *refs):
    x = place_ref[2]
    halves, out_ref, part_ref, sums_ref = (refs[:4], refs[4:8]), *refs[8:]
    for k in range(NX):
        line = jnp.zeros((1, 128), F32)
        for h in range(2):
            rows = wide_rows(halves[h][k])
            part_ref[2 * (k ^ x) + h, 0:128, :] = dot(rows, out_ref[...], ((1,), (1,))).astype(B16)
            for z in range(NZ):
                block = halves[h][k][z].astype(F32)
                line += jnp.sum(block * block, axis=0, keepdims=True)
        sums_ref[k ^ x] = line
    total = sums_ref[0] + sums_ref[1] + sums_ref[2] + sums_ref[3]
    top = total.astype(B16).astype(F32)
    middle = (total - top).astype(B16).astype(F32)
    bottom = total - top - middle
    row = lax.broadcasted_iota(jnp.int32, (16, 128), 0)
    lines = jnp.where(row == 0, top, jnp.where(row == 1, middle, jnp.where(row == 2, bottom, 0.0)))
    squares = lines.astype(B16)
    for gs in range(NY):
        part_ref[gs, 128:144, :] = squares


def weight_kernel(place_ref, *refs):
    x = place_ref[2]
    halves, heads_ref, weight_ref = (refs[:4], refs[4:8]), *refs[8:]
    total = jnp.zeros((128, COLS), F32)
    for k in range(NX):
        for h in range(2):
            total += dot(heads_ref[2 * (k ^ x) + h], wide_rows(halves[h][k]), ((0,), (0,)))
    weight_ref[...] = total.astype(B16)


def heads_parts(place, gathered, out_cols):
    specs = [whole(NZ, 128, 128)] * 8 + [whole(128, COLS)]
    outs = [jax.ShapeDtypeStruct((NY, 144, 128), B16)]
    return call(heads_kernel, specs, outs, 2 * 1024 * 1024 * 128, [pltpu.VMEM((NX, 1, 128), F32)])(
        place, *gathered, out_cols
    )[0]


def weight_grad(place, gathered, heads):
    specs = [whole(NZ, 128, 128)] * 8 + [whole(NY, 128, 128)]
    outs = [jax.ShapeDtypeStruct((128, COLS), B16)]
    return call(weight_kernel, specs, outs, 2 * 1024 * 1024 * 128)(place, *gathered, heads)[0]


def local(
    teacher_heads,
    teacher_out,
    teacher_resid,
    matches,
    projector,
    student_heads,
    student_out,
    student_resid,
):
    seq = lax.axis_index("seq")
    x = lax.axis_index("x")
    member = lax.axis_index(COLUMN)
    place = jnp.stack([member, seq, x, lax.axis_index(PLANE)]).astype(jnp.int32)
    swap = [(0, 1), (1, 0)]

    there = lax.ppermute(teacher_heads, "seq", swap)
    first = teacher_parts(place, teacher_heads, teacher_out)
    second = teacher_parts(place, there, teacher_out)

    *first, later = lax.optimization_barrier((*first, member))
    away = lax.dynamic_slice(projector, (0, (later + 1 - 2 * seq) * COLS), (256, COLS))
    other = lax.ppermute(away, "seq", swap)
    home = lax.dynamic_slice(projector, (0, later * COLS), (256, COLS))
    out_cols = lax.dynamic_slice(student_out, (0, later * COLS), (128, COLS))

    own_matches = lax.dynamic_slice(matches, (seq * 128,), (128,)).astype(B16)
    shared = jnp.concatenate([student_heads, jnp.broadcast_to(own_matches[None], (16, 128))], axis=0)
    resid_parts = jnp.transpose(student_resid.reshape(4, NY, 8, 128), (1, 0, 2, 3)).reshape(NY, 32, 128)
    early = jnp.concatenate([jnp.broadcast_to(shared[None], (NY,) + shared.shape), resid_parts], axis=1)
    early = lax.all_to_all(early, COLUMN, 0, 0)

    first, second, other, early = reduce_x(first, second, (other, early))

    heads = early[:, :128]
    picked = lax.dynamic_slice(early[:, 128], (2 * x, 0), (2, 128)).astype(jnp.int32).reshape(1, 256)
    partial = student_parts(place, heads, early[:, 144:].reshape(32, COLS), out_cols)
    first, partial, home = lax.optimization_barrier((first, partial, home))
    student_sum = lax.psum_scatter(partial, "x", scatter_dimension=0)
    student_sum = lax.psum_scatter(student_sum, "z", scatter_dimension=0)

    near = lax.dynamic_slice(teacher_resid, (seq * 64, 0), (64, 256))
    far = lax.dynamic_slice(teacher_resid, (64 - seq * 64, 0), (64, 256))
    moved = lax.all_to_all(jnp.concatenate([first, second], axis=1), "z", 0, 0)
    summed = jnp.sum(moved.astype(F32), axis=0)
    hidden = (jnp.concatenate([near, far], axis=0).astype(F32) + summed).astype(B16)

    got = lax.all_to_all(jnp.broadcast_to(hidden[None], (NY, 128, 256)), COLUMN, 0, 0)
    first, second = reduce_x(*projected_parts(place, got, home, other))
    moved = lax.all_to_all(jnp.concatenate([first, second], axis=1), "z", 0, 0)
    grad = gradient_piece(place, moved, student_sum, picked)

    tall = lax.all_to_all(grad, "z", 0, 0)
    gathered = gather_x(tall[:, :128], tall[:, 128:])

    sent = heads_parts(place, gathered, out_cols)
    back = lax.all_to_all(sent, COLUMN, 0, 0).astype(F32)
    grad_weight = weight_grad(place, gathered, heads)
    grad_heads = jnp.sum(back[:, :128], axis=0).astype(B16)
    total = jnp.sum(back[:, 128:])
    loss = (total * (64.0 / (ROWS * 8192))).reshape(1)
    return (loss, grad_heads, grad_weight)


def solution(mesh):
    cut = Mesh(mesh.devices.reshape(2, 2, 2, NZ, NX), COLUMN + PLANE)
    every = COLUMN + PLANE
    return jax.shard_map(
        local,
        mesh=cut,
        in_specs=(
            P(COLUMN, PLANE),
            P(PLANE, "seq"),
            P(GROUP, ("seq",) + PLANE),
            P(GROUP),
            P(("seq",) + PLANE, None),
            P(COLUMN, PLANE),
            P(PLANE, None),
            P(every, None),
        ),
        out_specs=(P(), P(COLUMN, PLANE), P(PLANE, COLUMN)),
        check_vma=False,
    )
```

```python
import functools

import jax
import jax.numpy as jnp
from jax import lax
from jax.experimental import pallas as pl
from jax.experimental.pallas import tpu as pltpu
from jax.sharding import Mesh, PartitionSpec as P

B16 = jnp.bfloat16
F32 = jnp.float32
NY, NZ, NX = 8, 8, 4
GROUP = ("ylo", "core")
COLUMN = ("ylo", "core", "seq")
PLANE = ("z", "x")
ROWS = 1024
COLS = 1024
HALF = COLS // 2
PARAMS = pltpu.CompilerParams(vmem_limit_bytes=32 * 1024 * 1024)


def dot(a, b, dims):
    return lax.dot_general(a, b, (dims, ((), ())), preferred_element_type=F32)


def add(*terms):
    total = terms[0].astype(F32)
    for term in terms[1:]:
        total += term.astype(F32)
    return total.astype(B16)


def across(block, flip):
    return lax.ppermute(block, "x", [(i, i ^ flip) for i in range(NX)])


def reduce_x(first, second, tie=()):
    first_far = across(first[2], 1)
    second_far = across(second[2], 3)
    first_near = across(first[1], 1)
    second_near = across(second[3], 3)
    if tie:
        first_far, second_far, *tie = lax.optimization_barrier((first_far, second_far, *tie))
    first_last = across(add(first[3], first_far), 3)
    second_last = across(add(second[1], second_far), 1)
    return (
        add(first[0], first_near, first_last),
        add(second[0], second_near, second_last),
        *tie,
    )


def gather_x(first, second):
    first_three = across(first, 3)
    second_one = across(second, 1)
    first_one = across(first, 1)
    second_three = across(second, 3)
    first_two = across(first_three, 1)
    second_two = across(second_one, 3)
    return first, first_one, first_two, first_three, second, second_one, second_two, second_three


def reduce_z(parts):
    moved = lax.all_to_all(parts, "z", 0, 0)
    return jnp.sum(moved.astype(F32), axis=0)


def own_order(rows):
    rest = rows.shape[2:]
    parts = rows.reshape((NY, NZ, NX, 4) + rest)
    return jnp.transpose(parts, (2, 1, 0, 3) + tuple(range(4, parts.ndim))).reshape((ROWS,) + rest)


def block_order(rows):
    rest = rows.shape[1:]
    parts = rows.reshape((NX, NZ, NY, 4) + rest)
    return jnp.transpose(parts, (2, 1, 0, 3) + tuple(range(4, parts.ndim))).reshape((NY, 128) + rest)


def whole(*shape):
    return pl.BlockSpec(shape, lambda i, m: (0,) * len(shape))


def call(kernel, in_specs, outs, flops, scratch=()):
    return pl.pallas_call(
        kernel,
        grid_spec=pltpu.PrefetchScalarGridSpec(
            num_scalar_prefetch=1,
            grid=(1,),
            in_specs=in_specs,
            out_specs=[whole(*out.shape) for out in outs],
            scratch_shapes=scratch,
        ),
        out_shape=outs,
        compiler_params=PARAMS,
        cost_estimate=pl.CostEstimate(flops=flops, bytes_accessed=5 << 20, transcendentals=0),
    )


def teacher_kernel(place_ref, rows_ref, out_ref, *refs):
    x = place_ref[2]
    parts, held, sems = refs[:NX], refs[NX], refs[NX + 1]
    copies = [
        pltpu.make_async_copy(out_ref.at[:, pl.ds(z * 1024, 1024)], held.at[z], sems.at[z]) for z in range(NZ)
    ]
    for copy in copies:
        copy.start()
    rows = rows_ref[...]
    for z in range(NZ):
        copies[z].wait()
        for k in range(NX):
            columns = pl.ds(pl.multiple_of((k ^ x) * 256, 256), 256)
            parts[k][z] = dot(rows, held[z, :, columns], ((1,), (0,))).astype(B16)


def teacher_parts(place, rows, teacher_out):
    outs = [jax.ShapeDtypeStruct((NZ, 64, 256), B16)] * NX
    scratch = [pltpu.VMEM((NZ, 256, 1024), B16), pltpu.SemaphoreType.DMA((NZ,))]
    specs = [whole(64, 256), pl.BlockSpec(memory_space=pltpu.HBM)]
    return call(teacher_kernel, specs, outs, 2 * 64 * 256 * 8192, scratch)(place, rows, teacher_out)


def gather_hidden(place_ref, got_ref, hidden_ref):
    seq = place_ref[1]
    for g in range(4):
        near = pl.ds(pl.multiple_of(g * 128 + seq * 64, 64), 64)
        far = pl.ds(pl.multiple_of(g * 128 + 64 - seq * 64, 64), 64)
        hidden_ref[near, 0:256] = got_ref[2 * g + seq, 0:64, :]
        hidden_ref[far, 0:256] = got_ref[2 * g + seq, 64:128, :]
        hidden_ref[far, 256:512] = got_ref[2 * g + 1 - seq, 0:64, :]
        hidden_ref[near, 256:512] = got_ref[2 * g + 1 - seq, 64:128, :]


def combine_kernel(jobs, place_ref, picked_ref, got_ref, heads_ref, out_ref, home_ref, other_ref, *refs):
    x = place_ref[2]
    parts, hidden_ref = refs[:-1], refs[-1]
    gather_hidden(place_ref, got_ref, hidden_ref)
    row = lax.broadcasted_iota(jnp.int32, (512, 256), 0)
    for k, halves in jobs:
        choose = (row == picked_ref[k ^ x]).astype(F32).astype(B16)
        selected = dot(choose, hidden_ref[...], ((0,), (0,))).astype(B16)
        heads = heads_ref[k ^ x]
        for half, to in halves:
            columns = slice(half * HALF, (half + 1) * HALF)
            total = dot(heads, out_ref[:, columns], ((1,), (0,)))
            total -= dot(selected[:, :256], home_ref[:, columns], ((1,), (0,)))
            total -= dot(selected[:, 256:], other_ref[:, columns], ((1,), (0,)))
            parts[to][...] = total.astype(B16)


SENT = ((2, ((0, 1), (1, 2))), (1, ((0, 0),)), (3, ((1, 3),)))
KEPT = ((3, ((0, 1),)), (1, ((1, 3),)), (0, ((0, 0), (1, 2))))


def combined_parts(jobs, place, picked, got, heads, out_cols, home, other):
    specs = [
        whole(NX, 1, 256),
        whole(NY, 128, 256),
        whole(NX, 256, 128),
        whole(128, COLS),
        whole(256, COLS),
        whole(256, COLS),
    ]
    outs = [jax.ShapeDtypeStruct((256, HALF), B16)] * 4
    return call(
        functools.partial(combine_kernel, jobs), specs, outs, 2 * 512 * 1024 * 900, [pltpu.VMEM((512, 512), B16)]
    )(place, picked, got, heads, out_cols, home, other)


def final_kernel(place_ref, *refs):
    x = place_ref[2]
    first, second = refs[:4], refs[4:8]
    out_ref, heads_ref, part_ref, squares_ref, weight_ref, sums_ref = refs[8:]
    left = jnp.zeros((128, HALF), F32)
    right = jnp.zeros((128, HALF), F32)
    for k in range(NX):
        near, far = first[k][...], second[k][...]
        part = dot(near, out_ref[:, :HALF], ((1,), (1,))) + dot(far, out_ref[:, HALF:], ((1,), (1,)))
        part_ref[k ^ x] = part.astype(B16)
        heads = heads_ref[k ^ x]
        left += dot(heads, near, ((0,), (0,)))
        right += dot(heads, far, ((0,), (0,)))
        near, far = near.astype(F32), far.astype(F32)
        line = jnp.sum(near * near + far * far, axis=0, keepdims=True)
        sums_ref[k ^ x] = line[:, :128] + line[:, 128:256] + line[:, 256:384] + line[:, 384:]
    weight_ref[:, :HALF] = left.astype(B16)
    weight_ref[:, HALF:] = right.astype(B16)
    total = sums_ref[0] + sums_ref[1] + sums_ref[2] + sums_ref[3]
    top = total.astype(B16).astype(F32)
    middle = (total - top).astype(B16).astype(F32)
    bottom = total - top - middle
    row = lax.broadcasted_iota(jnp.int32, (16, 128), 0)
    lines = jnp.where(row == 0, top, jnp.where(row == 1, middle, jnp.where(row == 2, bottom, 0.0)))
    squares_ref[...] = lines.astype(B16)


def final_parts(place, gathered, out_cols, heads):
    specs = [whole(256, HALF)] * 8 + [whole(128, COLS), whole(NX, 256, 128)]
    outs = [
        jax.ShapeDtypeStruct((NX, 256, 128), B16),
        jax.ShapeDtypeStruct((16, 128), B16),
        jax.ShapeDtypeStruct((128, COLS), B16),
    ]
    return call(final_kernel, specs, outs, 2 * 1024 * 1024 * 256, [pltpu.VMEM((NX, 1, 128), F32)])(
        place, *gathered, out_cols, heads
    )


def local(
    teacher_heads,
    teacher_out,
    teacher_resid,
    matches,
    projector,
    student_heads,
    student_out,
    student_resid,
):
    seq = lax.axis_index("seq")
    member = lax.axis_index(COLUMN)
    place = jnp.stack([member, seq, lax.axis_index("x")]).astype(jnp.int32)
    swap = [(0, 1), (1, 0)]

    there = lax.ppermute(teacher_heads, "seq", swap)
    first = teacher_parts(place, teacher_heads, teacher_out)
    second = teacher_parts(place, there, teacher_out)
    *second, later = lax.optimization_barrier((*second, member))

    own_matches = lax.dynamic_slice(matches, (later % 2 * 128,), (128,)).astype(B16)
    shared = jnp.concatenate([student_heads, jnp.broadcast_to(own_matches[None], (16, 128))], axis=0)
    resid_parts = jnp.transpose(student_resid.reshape(4, NY, 8, 128), (1, 0, 2, 3)).reshape(NY, 32, 128)
    early = jnp.concatenate([jnp.broadcast_to(shared[None], (NY,) + shared.shape), resid_parts], axis=1)
    early = lax.all_to_all(early, COLUMN, 0, 0)

    away = lax.dynamic_slice(projector, (0, (later + 1 - 2 * seq) * COLS), (256, COLS))
    other = lax.ppermute(away, "seq", swap)
    home = lax.dynamic_slice(projector, (0, later * COLS), (256, COLS))
    out_cols = lax.dynamic_slice(student_out, (0, later * COLS), (128, COLS))

    first, second, early = reduce_x(first, second, (early,))
    moved = lax.all_to_all(jnp.concatenate([first, second], axis=1), "z", 0, 0)
    moved, other = lax.optimization_barrier((moved, other))
    heads = own_order(early[:, :128]).reshape(NX, 256, 128)
    base = (jnp.arange(NY, dtype=jnp.int32) // 2 * 128)[:, None]
    picked = own_order(early[:, 128].astype(jnp.int32) + base).reshape(NX, 1, 256)
    resid = early[:, 144:].reshape(32, 2, HALF)
    resid = jnp.concatenate([resid[:, 0], resid[:, 1]], axis=0)
    near = lax.dynamic_slice(teacher_resid, (seq * 64, 0), (64, 256))
    far = lax.dynamic_slice(teacher_resid, (64 - seq * 64, 0), (64, 256))
    hidden = (jnp.concatenate([near, far], axis=0).astype(F32) + jnp.sum(moved.astype(F32), axis=0)).astype(B16)

    got = lax.all_to_all(jnp.broadcast_to(hidden[None], (NY, 128, 256)), COLUMN, 0, 0)
    operands = (place, picked, got, heads, out_cols, home, other)
    sent = combined_parts(SENT, *operands)
    kept = combined_parts(KEPT, *operands)
    sent = [part.reshape(NZ, 32, HALF) for part in sent]
    kept = [part.reshape(NZ, 32, HALF) for part in kept]
    first, second = reduce_x(
        (kept[0], sent[0], sent[1], kept[1]), (kept[2], kept[3], sent[2], sent[3])
    )
    summed = reduce_z(jnp.concatenate([first, second], axis=1))
    difference = resid.astype(F32) + summed
    grad = (difference * 0.125).astype(B16)

    tall = lax.all_to_all(jnp.broadcast_to(grad[None], (NZ, 64, HALF)), "z", 0, 0)
    gathered = gather_x(tall[:, :32].reshape(256, HALF), tall[:, 32:].reshape(256, HALF))

    heads_part, squares, grad_weight = final_parts(place, gathered, out_cols, heads)
    sent = jnp.concatenate(
        [block_order(heads_part.reshape(ROWS, 128)), jnp.broadcast_to(squares[None], (NY, 16, 128))], axis=1
    )
    back = lax.all_to_all(sent, COLUMN, 0, 0).astype(F32)
    grad_heads = jnp.sum(back[:, :128], axis=0).astype(B16)
    total = jnp.sum(back[:, 128:])
    loss = (total * (64.0 / (ROWS * 8192))).reshape(1)
    return (loss, grad_heads, grad_weight)


def solution(mesh):
    cut = Mesh(mesh.devices.reshape(2, 2, 2, NZ, NX), COLUMN + PLANE)
    every = COLUMN + PLANE
    return jax.shard_map(
        local,
        mesh=cut,
        in_specs=(
            P(COLUMN, PLANE),
            P(PLANE, "seq"),
            P(GROUP, ("seq",) + PLANE),
            P(GROUP),
            P(("seq",) + PLANE, None),
            P(COLUMN, PLANE),
            P(PLANE, None),
            P(every, None),
        ),
        out_specs=(P(), P(COLUMN, PLANE), P(PLANE, COLUMN)),
        check_vma=False,
    )
```

```python
import functools

import jax
import jax.numpy as jnp
from jax import lax
from jax.experimental import pallas as pl
from jax.experimental.pallas import tpu as pltpu
from jax.sharding import Mesh, PartitionSpec as P

B16 = jnp.bfloat16
F32 = jnp.float32
NY, NZ, NX = 8, 8, 4
GROUP = ("ylo", "core")
COLUMN = ("ylo", "core", "seq")
PLANE = ("z", "x")
ROWS = 1024
COLS = 1024
HALF = COLS // 2


def dot(a, b, dims):
    return lax.dot_general(a, b, (dims, ((), ())), preferred_element_type=F32)


def add(*terms):
    total = terms[0].astype(F32)
    for term in terms[1:]:
        total += term.astype(F32)
    return total.astype(B16)


def across(block, flip):
    return lax.ppermute(block, "x", [(i, i ^ flip) for i in range(NX)])


def reduce_x(first, second, tie=()):
    first_far = across(first[2], 1)
    second_far = across(second[2], 3)
    first_near = across(first[1], 1)
    second_near = across(second[3], 3)
    first_last = across(add(first[3], first_far), 3)
    second_last = across(add(second[1], second_far), 1)
    if tie:
        second_last, *tie = lax.optimization_barrier((second_last, *tie))
    return (
        add(first[0], first_near, first_last),
        add(second[0], second_near, second_last),
        *tie,
    )


def gather_x(first, second):
    first_three = across(first, 3)
    second_one = across(second, 1)
    first_one = across(first, 1)
    second_three = across(second, 3)
    first_two = across(first_three, 1)
    second_two = across(second_one, 3)
    return first, first_one, first_two, first_three, second, second_one, second_two, second_three


def reduce_z(parts):
    moved = lax.all_to_all(parts, "z", 0, 0)
    return jnp.sum(moved.astype(F32), axis=0)


def own_order(rows):
    rest = rows.shape[2:]
    parts = rows.reshape((NY, NZ, NX, 4) + rest)
    return jnp.transpose(parts, (2, 1, 0, 3) + tuple(range(4, parts.ndim))).reshape((ROWS,) + rest)


def block_order(rows):
    rest = rows.shape[1:]
    parts = rows.reshape((NX, NZ, NY, 4) + rest)
    return jnp.transpose(parts, (2, 1, 0, 3) + tuple(range(4, parts.ndim))).reshape((NY, 128) + rest)


def whole(*shape):
    return pl.BlockSpec(shape, lambda i, m: (0,) * len(shape))


def call(kernel, in_specs, outs, flops, scratch=(), limit=32):
    return pl.pallas_call(
        kernel,
        grid_spec=pltpu.PrefetchScalarGridSpec(
            num_scalar_prefetch=1,
            grid=(1,),
            in_specs=in_specs,
            out_specs=[whole(*out.shape) for out in outs],
            scratch_shapes=scratch,
        ),
        out_shape=outs,
        compiler_params=pltpu.CompilerParams(vmem_limit_bytes=limit << 20),
        cost_estimate=pl.CostEstimate(flops=flops, bytes_accessed=5 << 20, transcendentals=0),
    )


def teacher_kernel(place_ref, rows_ref, out_ref, *refs):
    x = place_ref[2]
    parts, held, sems = refs[:NX], refs[NX], refs[NX + 1]
    copies = [
        pltpu.make_async_copy(out_ref.at[:, pl.ds(z * 1024, 1024)], held.at[z], sems.at[z]) for z in range(NZ)
    ]
    for copy in copies:
        copy.start()
    rows = rows_ref[...]
    for z in range(NZ):
        copies[z].wait()
        for k in range(NX):
            columns = pl.ds(pl.multiple_of((k ^ x) * 256, 256), 256)
            parts[k][z] = dot(rows, held[z, :, columns], ((1,), (0,))).astype(B16)


def teacher_parts(place, rows, teacher_out):
    outs = [jax.ShapeDtypeStruct((NZ, 64, 256), B16)] * NX
    scratch = [pltpu.VMEM((NZ, 256, 1024), B16), pltpu.SemaphoreType.DMA((NZ,))]
    specs = [whole(64, 256), pl.BlockSpec(memory_space=pltpu.HBM)]
    return call(teacher_kernel, specs, outs, 2 * 64 * 256 * 8192, scratch, 57)(place, rows, teacher_out)


def gather_hidden(place_ref, got_ref, hidden_ref):
    seq = place_ref[1]
    for g in range(4):
        near = pl.ds(pl.multiple_of(g * 128 + seq * 64, 64), 64)
        far = pl.ds(pl.multiple_of(g * 128 + 64 - seq * 64, 64), 64)
        for c in range(2):
            at, home, other = c * 128, slice(c * 128, c * 128 + 128), slice(256 + c * 128, 384 + c * 128)
            hidden_ref[near, home] = got_ref[2 * g + seq, at : at + 64, :]
            hidden_ref[far, home] = got_ref[2 * g + seq, at + 64 : at + 128, :]
            hidden_ref[far, other] = got_ref[2 * g + 1 - seq, at : at + 64, :]
            hidden_ref[near, other] = got_ref[2 * g + 1 - seq, at + 64 : at + 128, :]


def combine_kernel(jobs, place_ref, picked_ref, got_ref, heads_ref, out_ref, home_ref, other_ref, *refs):
    x = place_ref[2]
    parts, hidden_ref = refs[:-1], refs[-1]
    gather_hidden(place_ref, got_ref, hidden_ref)
    row = lax.broadcasted_iota(jnp.int32, (512, 256), 0)
    for k, halves in jobs:
        choose = (row == picked_ref[k ^ x]).astype(F32).astype(B16)
        selected = dot(choose, hidden_ref[...], ((0,), (0,))).astype(B16)
        heads = heads_ref[k ^ x]
        for half, to in halves:
            columns = slice(half * HALF, (half + 1) * HALF)
            total = dot(heads, out_ref[:, columns], ((1,), (0,)))
            total -= dot(selected[:, :256], home_ref[:, columns], ((1,), (0,)))
            total -= dot(selected[:, 256:], other_ref[:, columns], ((1,), (0,)))
            parts[to][...] = total.astype(B16)


SENT = ((2, ((0, 1), (1, 2))), (1, ((0, 0),)), (3, ((1, 3),)))
KEPT = ((3, ((0, 1),)), (1, ((1, 3),)), (0, ((0, 0), (1, 2))))


def combined_parts(jobs, place, picked, got, heads, student_out, projector, other):
    specs = [
        whole(NX, 1, 256),
        whole(NY, 432, 128),
        whole(NX, 256, 128),
        pl.BlockSpec((128, COLS), lambda i, m: (0, m[0])),
        pl.BlockSpec((256, COLS), lambda i, m: (0, m[0])),
        whole(256, COLS),
    ]
    outs = [jax.ShapeDtypeStruct((256, HALF), B16)] * 4
    return call(
        functools.partial(combine_kernel, jobs), specs, outs, 2 * 512 * 1024 * 900, [pltpu.VMEM((512, 512), B16)], 57
    )(place, picked, got, heads, student_out, projector, other)


def final_kernel(place_ref, *refs):
    x = place_ref[2]
    first, second = refs[:4], refs[4:8]
    out_ref, heads_ref, part_ref, squares_ref, weight_ref, sums_ref = refs[8:]
    left = jnp.zeros((128, HALF), F32)
    right = jnp.zeros((128, HALF), F32)
    for k in range(NX):
        near, far = first[k][...], second[k][...]
        part = dot(near, out_ref[:, :HALF], ((1,), (1,))) + dot(far, out_ref[:, HALF:], ((1,), (1,)))
        part_ref[k ^ x] = part.astype(B16)
        heads = heads_ref[k ^ x]
        left += dot(heads, near, ((0,), (0,)))
        right += dot(heads, far, ((0,), (0,)))
        near, far = near.astype(F32), far.astype(F32)
        line = jnp.sum(near * near + far * far, axis=0, keepdims=True)
        sums_ref[k ^ x] = line[:, :128] + line[:, 128:256] + line[:, 256:384] + line[:, 384:]
    weight_ref[:, :HALF] = left.astype(B16)
    weight_ref[:, HALF:] = right.astype(B16)
    total = sums_ref[0] + sums_ref[1] + sums_ref[2] + sums_ref[3]
    top = total.astype(B16).astype(F32)
    middle = (total - top).astype(B16).astype(F32)
    bottom = total - top - middle
    row = lax.broadcasted_iota(jnp.int32, (16, 128), 0)
    lines = jnp.where(row == 0, top, jnp.where(row == 1, middle, jnp.where(row == 2, bottom, 0.0)))
    squares_ref[...] = lines.astype(B16)


def final_parts(place, gathered, student_out, heads):
    specs = [whole(256, HALF)] * 8 + [pl.BlockSpec((128, COLS), lambda i, m: (0, m[0])), whole(NX, 256, 128)]
    outs = [
        jax.ShapeDtypeStruct((NX, 256, 128), B16),
        jax.ShapeDtypeStruct((16, 128), B16),
        jax.ShapeDtypeStruct((128, COLS), B16),
    ]
    return call(final_kernel, specs, outs, 2 * 1024 * 1024 * 256, [pltpu.VMEM((NX, 1, 128), F32)])(
        place, *gathered, student_out, heads
    )


def local(
    teacher_heads,
    teacher_out,
    teacher_resid,
    matches,
    projector,
    student_heads,
    student_out,
    student_resid,
):
    seq = lax.axis_index("seq")
    member = lax.axis_index(COLUMN)
    place = jnp.stack([member, seq, lax.axis_index("x")]).astype(jnp.int32)
    swap = [(0, 1), (1, 0)]

    there = lax.ppermute(teacher_heads, "seq", swap)
    first = list(teacher_parts(place, teacher_heads, teacher_out))
    first[2], there = lax.optimization_barrier((first[2], there))
    second = list(teacher_parts(place, there, teacher_out))

    second[2], later = lax.optimization_barrier((second[2], member))
    away = lax.dynamic_slice(projector, (0, (later + 1 - 2 * seq) * COLS), (256, COLS))
    other = lax.ppermute(away, "seq", swap)

    first, second, other = reduce_x(first, second, (other,))
    moved = lax.all_to_all(jnp.concatenate([first, second], axis=1), "z", 0, 0)
    near = lax.dynamic_slice(teacher_resid, (seq * 64, 0), (64, 256))
    far = lax.dynamic_slice(teacher_resid, (64 - seq * 64, 0), (64, 256))
    hidden = (jnp.concatenate([near, far], axis=0).astype(F32) + jnp.sum(moved.astype(F32), axis=0)).astype(B16)

    own_matches = lax.dynamic_slice(matches, (seq * 128,), (128,)).astype(B16)
    shared = jnp.concatenate(
        [hidden[:, :128], hidden[:, 128:], student_heads, jnp.broadcast_to(own_matches[None], (16, 128))], axis=0
    )
    resid_parts = jnp.transpose(student_resid.reshape(4, NY, 8, 128), (1, 0, 2, 3)).reshape(NY, 32, 128)
    sent = jnp.concatenate([jnp.broadcast_to(shared[None], (NY,) + shared.shape), resid_parts], axis=1)
    got = lax.all_to_all(sent, COLUMN, 0, 0)
    heads = own_order(got[:, 256:384]).reshape(NX, 256, 128)
    base = (jnp.arange(NY, dtype=jnp.int32) // 2 * 128)[:, None]
    picked = own_order(got[:, 384].astype(jnp.int32) + base).reshape(NX, 1, 256)
    operands = (place, picked, got, heads, student_out, projector, other)
    sent = combined_parts(SENT, *operands)
    kept = combined_parts(KEPT, *operands)
    sent = [part.reshape(NZ, 32, HALF) for part in sent]
    kept = [part.reshape(NZ, 32, HALF) for part in kept]
    resid = got[:, 400:].reshape(32, 2, HALF)
    resid = jnp.concatenate([resid[:, 0], resid[:, 1]], axis=0)
    first, second = reduce_x(
        (kept[0], sent[0], sent[1], kept[1]), (kept[2], kept[3], sent[2], sent[3])
    )
    summed = reduce_z(jnp.concatenate([first, second], axis=1))
    difference = resid.astype(F32) + summed
    grad = (difference * 0.125).astype(B16)

    tall = lax.all_to_all(jnp.broadcast_to(grad[None], (NZ, 64, HALF)), "z", 0, 0)
    gathered = gather_x(tall[:, :32].reshape(256, HALF), tall[:, 32:].reshape(256, HALF))

    heads_part, squares, grad_weight = final_parts(place, gathered, student_out, heads)
    sent = jnp.concatenate(
        [block_order(heads_part.reshape(ROWS, 128)), jnp.broadcast_to(squares[None], (NY, 16, 128))], axis=1
    )
    back = lax.all_to_all(sent, COLUMN, 0, 0).astype(F32)
    grad_heads = jnp.sum(back[:, :128], axis=0).astype(B16)
    total = jnp.sum(back[:, 128:])
    loss = (total * (64.0 / (ROWS * 8192))).reshape(1)
    return (loss, grad_heads, grad_weight)


def solution(mesh):
    cut = Mesh(mesh.devices.reshape(2, 2, 2, NZ, NX), COLUMN + PLANE)
    every = COLUMN + PLANE
    return jax.shard_map(
        local,
        mesh=cut,
        in_specs=(
            P(COLUMN, PLANE),
            P(PLANE, "seq"),
            P(GROUP, ("seq",) + PLANE),
            P(GROUP),
            P(("seq",) + PLANE, None),
            P(COLUMN, PLANE),
            P(PLANE, None),
            P(every, None),
        ),
        out_specs=(P(), P(COLUMN, PLANE), P(PLANE, COLUMN)),
        check_vma=False,
    )
```

```python
import functools

import jax
import jax.numpy as jnp
from jax import lax
from jax.experimental import pallas as pl
from jax.experimental.pallas import tpu as pltpu
from jax.sharding import Mesh, PartitionSpec as P

B16 = jnp.bfloat16
F32 = jnp.float32
NY, NZ, NX = 8, 8, 4
GROUP = ("ylo", "core")
COLUMN = ("ylo", "core", "seq")
PLANE = ("z", "x")
ROWS = 1024
COLS = 1024
HALF = COLS // 2


def dot(a, b, dims):
    return lax.dot_general(a, b, (dims, ((), ())), preferred_element_type=F32)


def add(*terms):
    total = terms[0].astype(F32)
    for term in terms[1:]:
        total += term.astype(F32)
    return total.astype(B16)


def across(block, flip):
    return lax.ppermute(block, "x", [(i, i ^ flip) for i in range(NX)])


def reduce_x(place, first, second, tie=()):
    first_far = across(first[2], 1)
    second_far = across(second[2], 3)
    first_near = across(first[1], 1)
    second_near = across(second[3], 3)
    first_last = across(add(first[3], first_far), 3)
    second_last = across(add(second[1], second_far), 1)
    if tie:
        second_last, *tie = lax.optimization_barrier((second_last, *tie))
    return (merge(place, first[0], first_near, first_last, second[0], second_near, second_last), *tie)


def gather_x(first, second):
    first_three = across(first, 3)
    second_one = across(second, 1)
    first_one = across(first, 1)
    second_three = across(second, 3)
    first_two = across(first_three, 1)
    second_two = across(second_one, 3)
    return first, first_one, first_two, first_three, second, second_one, second_two, second_three


def reduce_z(parts):
    moved = lax.all_to_all(parts, "z", 0, 0)
    return jnp.sum(moved.astype(F32), axis=0)


def own_order(rows):
    rest = rows.shape[2:]
    parts = rows.reshape((NY, NZ, NX, 4) + rest)
    return jnp.transpose(parts, (2, 1, 0, 3) + tuple(range(4, parts.ndim))).reshape((ROWS,) + rest)


def block_order(rows):
    rest = rows.shape[1:]
    parts = rows.reshape((NX, NZ, NY, 4) + rest)
    return jnp.transpose(parts, (2, 1, 0, 3) + tuple(range(4, parts.ndim))).reshape((NY, 128) + rest)


def whole(*shape):
    return pl.BlockSpec(shape, lambda i, m: (0,) * len(shape))


def call(kernel, in_specs, outs, flops, scratch=(), limit=32):
    return pl.pallas_call(
        kernel,
        grid_spec=pltpu.PrefetchScalarGridSpec(
            num_scalar_prefetch=1,
            grid=(1,),
            in_specs=in_specs,
            out_specs=[whole(*out.shape) for out in outs],
            scratch_shapes=scratch,
        ),
        out_shape=outs,
        compiler_params=pltpu.CompilerParams(vmem_limit_bytes=limit << 20),
        cost_estimate=pl.CostEstimate(flops=flops, bytes_accessed=5 << 20, transcendentals=0),
    )


def multiply(rows, weights, z, x, parts):
    for k in range(NX):
        columns = pl.ds(pl.multiple_of((k ^ x) * 256, 256), 256)
        parts[k][z] = dot(rows, weights[z, :, columns], ((1,), (0,))).astype(B16)


def own_kernel(place_ref, rows_ref, out_ref, *refs):
    parts, held, sems = refs[:NX], refs[NX], refs[NX + 1]
    copies = [
        pltpu.make_async_copy(out_ref.at[:, pl.ds(z * 1024, 1024)], held.at[z], sems.at[z]) for z in range(NZ)
    ]
    for copy in copies:
        copy.start()
    rows = rows_ref[...]
    for z in range(NZ):
        copies[z].wait()
        multiply(rows, held, z, place_ref[2], parts)


def there_kernel(place_ref, rows_ref, held_ref, *parts):
    rows = rows_ref[...]
    for z in range(NZ):
        multiply(rows, held_ref, z, place_ref[2], parts)


PARTS = [jax.ShapeDtypeStruct((NZ, 64, 256), B16)] * NX


def own_parts(place, rows, teacher_out):
    specs = [whole(64, 256), pl.BlockSpec(memory_space=pltpu.HBM)]
    outs = PARTS + [jax.ShapeDtypeStruct((NZ, 256, 1024), B16)]
    *parts, held = call(own_kernel, specs, outs, 2 * 64 * 256 * 8192, [pltpu.SemaphoreType.DMA((NZ,))], 24)(
        place, rows, teacher_out
    )
    return parts, held


def there_parts(place, rows, held):
    specs = [whole(64, 256), whole(NZ, 256, 1024)]
    return list(call(there_kernel, specs, PARTS, 2 * 64 * 256 * 8192, (), 24)(place, rows, held))


def merge_kernel(place_ref, *refs):
    rows = refs[0].shape[1]
    for half in range(2):
        terms = refs[3 * half : 3 * half + 3]
        total = terms[0][...].astype(F32) + terms[1][...].astype(F32) + terms[2][...].astype(F32)
        refs[6][:, half * rows : (half + 1) * rows, :] = total.astype(B16)


def merge(place, *terms):
    n, rows, columns = terms[0].shape
    outs = [jax.ShapeDtypeStruct((n, 2 * rows, columns), B16)]
    return call(merge_kernel, [whole(n, rows, columns)] * 6, outs, 1 << 21, (), 16)(place, *terms)[0]


def layout_kernel(place_ref, home_in, other_in, out_in, weights_ref, out_ref):
    weights_ref[0:256, :] = home_in[...]
    weights_ref[256:512, :] = other_in[...]
    out_ref[...] = out_in[...]


def layout(place, projector, other, student_out):
    specs = [
        pl.BlockSpec((256, COLS), lambda i, m: (0, m[0])),
        whole(256, COLS),
        pl.BlockSpec((128, COLS), lambda i, m: (0, m[0])),
    ]
    outs = [jax.ShapeDtypeStruct((512, COLS), B16), jax.ShapeDtypeStruct((128, COLS), B16)]
    return call(layout_kernel, specs, outs, 1 << 21, (), 16)(place, projector, other, student_out)


def gather_hidden(place_ref, got_ref, hidden_ref):
    seq = place_ref[1]
    for g in range(4):
        near = pl.ds(pl.multiple_of(g * 128 + seq * 64, 64), 64)
        far = pl.ds(pl.multiple_of(g * 128 + 64 - seq * 64, 64), 64)
        for c in range(2):
            at, home, other = c * 128, slice(c * 128, c * 128 + 128), slice(256 + c * 128, 384 + c * 128)
            hidden_ref[near, home] = got_ref[2 * g + seq, at : at + 64, :]
            hidden_ref[far, home] = got_ref[2 * g + seq, at + 64 : at + 128, :]
            hidden_ref[far, other] = got_ref[2 * g + 1 - seq, at : at + 64, :]
            hidden_ref[near, other] = got_ref[2 * g + 1 - seq, at + 64 : at + 128, :]


def combine_kernel(jobs, place_ref, picked_ref, got_ref, heads_ref, out_ref, weights_ref, *refs):
    x = place_ref[2]
    parts, hidden_ref = refs[:-1], refs[-1]
    gather_hidden(place_ref, got_ref, hidden_ref)
    row = lax.broadcasted_iota(jnp.int32, (512, 256), 0)
    for k, halves in jobs:
        choose = (row == picked_ref[k ^ x]).astype(F32).astype(B16)
        selected = dot(choose, hidden_ref[...], ((0,), (0,))).astype(B16)
        heads = heads_ref[k ^ x]
        for half, to in halves:
            columns = slice(half * HALF, (half + 1) * HALF)
            total = dot(heads, out_ref[:, columns], ((1,), (0,)))
            total -= dot(selected, weights_ref[:, columns], ((1,), (0,)))
            parts[to][...] = total.astype(B16)


SENT = ((2, ((0, 1), (1, 2))), (1, ((0, 0),)), (3, ((1, 3),)))
KEPT = ((3, ((0, 1),)), (1, ((1, 3),)), (0, ((0, 0), (1, 2))))


def combined_parts(jobs, place, picked, got, heads, out_cols, weights):
    specs = [whole(NX, 1, 256), whole(NY, 432, 128), whole(NX, 256, 128), whole(128, COLS), whole(512, COLS)]
    outs = [jax.ShapeDtypeStruct((256, HALF), B16)] * 4
    return call(
        functools.partial(combine_kernel, jobs), specs, outs, 2 * 512 * 1024 * 900, [pltpu.VMEM((512, 512), B16)], 24
    )(place, picked, got, heads, out_cols, weights)


def final_kernel(place_ref, *refs):
    x = place_ref[2]
    first, second = refs[:4], refs[4:8]
    out_ref, heads_ref, part_ref, squares_ref, weight_ref, sums_ref = refs[8:]
    left = jnp.zeros((128, HALF), F32)
    right = jnp.zeros((128, HALF), F32)
    for k in range(NX):
        near, far = first[k][...], second[k][...]
        part = dot(near, out_ref[:, :HALF], ((1,), (1,))) + dot(far, out_ref[:, HALF:], ((1,), (1,)))
        part_ref[k ^ x] = part.astype(B16)
        heads = heads_ref[k ^ x]
        left += dot(heads, near, ((0,), (0,)))
        right += dot(heads, far, ((0,), (0,)))
        near, far = near.astype(F32), far.astype(F32)
        line = jnp.sum(near * near + far * far, axis=0, keepdims=True)
        sums_ref[k ^ x] = line[:, :128] + line[:, 128:256] + line[:, 256:384] + line[:, 384:]
    weight_ref[:, :HALF] = left.astype(B16)
    weight_ref[:, HALF:] = right.astype(B16)
    total = sums_ref[0] + sums_ref[1] + sums_ref[2] + sums_ref[3]
    top = total.astype(B16).astype(F32)
    middle = (total - top).astype(B16).astype(F32)
    bottom = total - top - middle
    row = lax.broadcasted_iota(jnp.int32, (16, 128), 0)
    lines = jnp.where(row == 0, top, jnp.where(row == 1, middle, jnp.where(row == 2, bottom, 0.0)))
    squares_ref[...] = lines.astype(B16)


def final_parts(place, gathered, student_out, heads):
    specs = [whole(256, HALF)] * 8 + [pl.BlockSpec((128, COLS), lambda i, m: (0, m[0])), whole(NX, 256, 128)]
    outs = [
        jax.ShapeDtypeStruct((NX, 256, 128), B16),
        jax.ShapeDtypeStruct((16, 128), B16),
        jax.ShapeDtypeStruct((128, COLS), B16),
    ]
    return call(final_kernel, specs, outs, 2 * 1024 * 1024 * 256, [pltpu.VMEM((NX, 1, 128), F32)])(
        place, *gathered, student_out, heads
    )


def local(
    teacher_heads,
    teacher_out,
    teacher_resid,
    matches,
    projector,
    student_heads,
    student_out,
    student_resid,
):
    seq = lax.axis_index("seq")
    member = lax.axis_index(COLUMN)
    place = jnp.stack([member, seq, lax.axis_index("x")]).astype(jnp.int32)
    swap = [(0, 1), (1, 0)]

    there = lax.ppermute(teacher_heads, "seq", swap)
    first, held = own_parts(place, teacher_heads, teacher_out)
    second = there_parts(place, there, held)

    second[2], later = lax.optimization_barrier((second[2], member))
    away = lax.dynamic_slice(projector, (0, (later + 1 - 2 * seq) * COLS), (256, COLS))
    other = lax.ppermute(away, "seq", swap)

    summed, other = reduce_x(place, first, second, (other,))
    moved = lax.all_to_all(summed, "z", 0, 0)
    near = lax.dynamic_slice(teacher_resid, (seq * 64, 0), (64, 256))
    far = lax.dynamic_slice(teacher_resid, (64 - seq * 64, 0), (64, 256))
    hidden = (jnp.concatenate([near, far], axis=0).astype(F32) + jnp.sum(moved.astype(F32), axis=0)).astype(B16)

    spot, hidden = lax.optimization_barrier((place, hidden))
    weights, out_cols = layout(spot, projector, other, student_out)

    own_matches = lax.dynamic_slice(matches, (seq * 128,), (128,)).astype(B16)
    shared = jnp.concatenate(
        [hidden[:, :128], hidden[:, 128:], student_heads, jnp.broadcast_to(own_matches[None], (16, 128))], axis=0
    )
    resid_parts = jnp.transpose(student_resid.reshape(4, NY, 8, 128), (1, 0, 2, 3)).reshape(NY, 32, 128)
    sent = jnp.concatenate([jnp.broadcast_to(shared[None], (NY,) + shared.shape), resid_parts], axis=1)
    got = lax.all_to_all(sent, COLUMN, 0, 0)
    heads = own_order(got[:, 256:384]).reshape(NX, 256, 128)
    base = (jnp.arange(NY, dtype=jnp.int32) // 2 * 128)[:, None]
    picked = own_order(got[:, 384].astype(jnp.int32) + base).reshape(NX, 1, 256)
    operands = (place, picked, got, heads, out_cols, weights)
    sent = combined_parts(SENT, *operands)
    kept = combined_parts(KEPT, *operands)
    sent = [part.reshape(NZ, 32, HALF) for part in sent]
    kept = [part.reshape(NZ, 32, HALF) for part in kept]
    resid = got[:, 400:].reshape(32, 2, HALF)
    resid = jnp.concatenate([resid[:, 0], resid[:, 1]], axis=0)
    (summed,) = reduce_x(
        place, (kept[0], sent[0], sent[1], kept[1]), (kept[2], kept[3], sent[2], sent[3])
    )
    summed = reduce_z(summed)
    difference = resid.astype(F32) + summed
    grad = (difference * 0.125).astype(B16)

    tall = lax.all_to_all(jnp.broadcast_to(grad[None], (NZ, 64, HALF)), "z", 0, 0)
    gathered = gather_x(tall[:, :32].reshape(256, HALF), tall[:, 32:].reshape(256, HALF))

    heads_part, squares, grad_weight = final_parts(place, gathered, student_out, heads)
    sent = jnp.concatenate(
        [block_order(heads_part.reshape(ROWS, 128)), jnp.broadcast_to(squares[None], (NY, 16, 128))], axis=1
    )
    back = lax.all_to_all(sent, COLUMN, 0, 0).astype(F32)
    grad_heads = jnp.sum(back[:, :128], axis=0).astype(B16)
    total = jnp.sum(back[:, 128:])
    loss = (total * (64.0 / (ROWS * 8192))).reshape(1)
    return (loss, grad_heads, grad_weight)


def solution(mesh):
    cut = Mesh(mesh.devices.reshape(2, 2, 2, NZ, NX), COLUMN + PLANE)
    every = COLUMN + PLANE
    return jax.shard_map(
        local,
        mesh=cut,
        in_specs=(
            P(COLUMN, PLANE),
            P(PLANE, "seq"),
            P(GROUP, ("seq",) + PLANE),
            P(GROUP),
            P(("seq",) + PLANE, None),
            P(COLUMN, PLANE),
            P(PLANE, None),
            P(every, None),
        ),
        out_specs=(P(), P(COLUMN, PLANE), P(PLANE, COLUMN)),
        check_vma=False,
    )
```

```python
import functools

import jax
import jax.numpy as jnp
from jax import lax
from jax.experimental import pallas as pl
from jax.experimental.pallas import tpu as pltpu
from jax.sharding import Mesh, PartitionSpec as P

B16 = jnp.bfloat16
F32 = jnp.float32
NY, NZ, NX = 8, 8, 4
GROUP = ("ylo", "core")
COLUMN = ("ylo", "core", "seq")
PLANE = ("z", "x")
ROWS = 1024
COLS = 1024
HALF = COLS // 2


def dot(a, b, dims):
    return lax.dot_general(a, b, (dims, ((), ())), preferred_element_type=F32)


def add(*terms):
    total = terms[0].astype(F32)
    for term in terms[1:]:
        total += term.astype(F32)
    return total.astype(B16)


def across(block, flip):
    return lax.ppermute(block, "x", [(i, i ^ flip) for i in range(NX)])


def reduce_x(first, second, before, tie=()):
    first_far = across(first[2], 1)
    second_far = across(second[2], 3)
    first_near, second_near, *before = lax.optimization_barrier((first[1], second[3], *before))
    first_near = across(first_near, 1)
    second_near = across(second_near, 3)
    first_last = across(add(first[3], first_far), 3)
    second_last = across(add(second[1], second_far), 1)
    if tie:
        second_last, *tie = lax.optimization_barrier((second_last, *tie))
    return (
        jnp.concatenate(
            [add(first[0], first_near, first_last), add(second[0], second_near, second_last)], axis=1
        ),
        *tie,
    )


def gather_x(first, second):
    first_three = across(first, 3)
    second_one = across(second, 1)
    first_one = across(first, 1)
    second_three = across(second, 3)
    first_two = across(first_three, 1)
    second_two = across(second_one, 3)
    return first, first_one, first_two, first_three, second, second_one, second_two, second_three


def reduce_z(parts):
    moved = lax.all_to_all(parts, "z", 0, 0)
    return jnp.sum(moved.astype(F32), axis=0)


def own_order(rows):
    rest = rows.shape[2:]
    parts = rows.reshape((NY, NZ, NX, 4) + rest)
    return jnp.transpose(parts, (2, 1, 0, 3) + tuple(range(4, parts.ndim))).reshape((ROWS,) + rest)


def block_order(rows):
    rest = rows.shape[1:]
    parts = rows.reshape((NX, NZ, NY, 4) + rest)
    return jnp.transpose(parts, (2, 1, 0, 3) + tuple(range(4, parts.ndim))).reshape((NY, 128) + rest)


def whole(*shape):
    return pl.BlockSpec(shape, lambda i, m: (0,) * len(shape))


def call(kernel, in_specs, outs, flops, scratch=(), limit=32):
    return pl.pallas_call(
        kernel,
        grid_spec=pltpu.PrefetchScalarGridSpec(
            num_scalar_prefetch=1,
            grid=(1,),
            in_specs=in_specs,
            out_specs=[whole(*out.shape) for out in outs],
            scratch_shapes=scratch,
        ),
        out_shape=outs,
        compiler_params=pltpu.CompilerParams(vmem_limit_bytes=limit << 20),
        cost_estimate=pl.CostEstimate(flops=flops, bytes_accessed=5 << 20, transcendentals=0),
    )


def multiply(rows, weights, z, x, parts):
    for k in range(NX):
        columns = pl.ds(pl.multiple_of((k ^ x) * 256, 256), 256)
        parts[k][z] = dot(rows, weights[z, :, columns], ((1,), (0,))).astype(B16)


def own_kernel(place_ref, rows_ref, out_ref, *refs):
    parts, held, sems = refs[:NX], refs[NX], refs[NX + 1]
    copies = [
        pltpu.make_async_copy(out_ref.at[:, pl.ds(z * 1024, 1024)], held.at[z], sems.at[z]) for z in range(NZ)
    ]
    for copy in copies:
        copy.start()
    rows = rows_ref[...]
    for z in range(NZ):
        copies[z].wait()
        multiply(rows, held, z, place_ref[2], parts)


def there_kernel(place_ref, rows_ref, held_ref, *parts):
    rows = rows_ref[...]
    for z in range(NZ):
        multiply(rows, held_ref, z, place_ref[2], parts)


PARTS = [jax.ShapeDtypeStruct((NZ, 64, 256), B16)] * NX


def own_parts(place, rows, teacher_out):
    specs = [whole(64, 256), pl.BlockSpec(memory_space=pltpu.HBM)]
    outs = PARTS + [jax.ShapeDtypeStruct((NZ, 256, 1024), B16)]
    *parts, held = call(own_kernel, specs, outs, 2 * 64 * 256 * 8192, [pltpu.SemaphoreType.DMA((NZ,))], 24)(
        place, rows, teacher_out
    )
    return parts, held


def there_parts(place, rows, held):
    specs = [whole(64, 256), whole(NZ, 256, 1024)]
    return list(call(there_kernel, specs, PARTS, 2 * 64 * 256 * 8192, (), 24)(place, rows, held))


def layout_kernel(place_ref, home_in, other_in, out_in, weights_ref, out_ref):
    weights_ref[0:256, :] = home_in[...]
    weights_ref[256:512, :] = other_in[...]
    out_ref[...] = out_in[...]


def layout(place, projector, other, student_out):
    specs = [
        pl.BlockSpec((256, COLS), lambda i, m: (0, m[0])),
        whole(256, COLS),
        pl.BlockSpec((128, COLS), lambda i, m: (0, m[0])),
    ]
    outs = [jax.ShapeDtypeStruct((512, COLS), B16), jax.ShapeDtypeStruct((128, COLS), B16)]
    return call(layout_kernel, specs, outs, 1 << 21, (), 16)(place, projector, other, student_out)


def gather_hidden(place_ref, got_ref, hidden_ref):
    seq = place_ref[1]
    for g in range(4):
        near = pl.ds(pl.multiple_of(g * 128 + seq * 64, 64), 64)
        far = pl.ds(pl.multiple_of(g * 128 + 64 - seq * 64, 64), 64)
        for c in range(2):
            at, home, other = c * 128, slice(c * 128, c * 128 + 128), slice(256 + c * 128, 384 + c * 128)
            hidden_ref[near, home] = got_ref[2 * g + seq, at : at + 64, :]
            hidden_ref[far, home] = got_ref[2 * g + seq, at + 64 : at + 128, :]
            hidden_ref[far, other] = got_ref[2 * g + 1 - seq, at : at + 64, :]
            hidden_ref[near, other] = got_ref[2 * g + 1 - seq, at + 64 : at + 128, :]


def combine_kernel(jobs, place_ref, picked_ref, got_ref, heads_ref, out_ref, weights_ref, *refs):
    x = place_ref[2]
    parts, hidden_ref = refs[:-1], refs[-1]
    gather_hidden(place_ref, got_ref, hidden_ref)
    row = lax.broadcasted_iota(jnp.int32, (512, 256), 0)
    for k, halves in jobs:
        choose = (row == picked_ref[k ^ x]).astype(F32).astype(B16)
        selected = dot(choose, hidden_ref[...], ((0,), (0,))).astype(B16)
        heads = heads_ref[k ^ x]
        for half, to in halves:
            columns = slice(half * HALF, (half + 1) * HALF)
            total = dot(heads, out_ref[:, columns], ((1,), (0,)))
            total -= dot(selected, weights_ref[:, columns], ((1,), (0,)))
            parts[to][...] = total.astype(B16)


FAR = ((2, ((0, 0), (1, 1))),)
REST = ((1, ((0, 0), (1, 3))), (3, ((1, 4), (0, 1))), (0, ((0, 2), (1, 5))))


def combined_parts(jobs, place, picked, got, heads, out_cols, weights):
    specs = [whole(NX, 1, 256), whole(NY, 432, 128), whole(NX, 256, 128), whole(128, COLS), whole(512, COLS)]
    count = sum(len(halves) for _, halves in jobs)
    outs = [jax.ShapeDtypeStruct((256, HALF), B16)] * count
    return call(
        functools.partial(combine_kernel, jobs), specs, outs, count * 2 * 256 * 512 * 900, [pltpu.VMEM((512, 512), B16)], 24
    )(place, picked, got, heads, out_cols, weights)


def final_kernel(place_ref, *refs):
    x = place_ref[2]
    first, second = refs[:4], refs[4:8]
    out_ref, heads_ref, part_ref, squares_ref, weight_ref, sums_ref = refs[8:]
    left = jnp.zeros((128, HALF), F32)
    right = jnp.zeros((128, HALF), F32)
    for k in range(NX):
        near, far = first[k][...], second[k][...]
        part = dot(near, out_ref[:, :HALF], ((1,), (1,))) + dot(far, out_ref[:, HALF:], ((1,), (1,)))
        part_ref[k ^ x] = part.astype(B16)
        heads = heads_ref[k ^ x]
        left += dot(heads, near, ((0,), (0,)))
        right += dot(heads, far, ((0,), (0,)))
        near, far = near.astype(F32), far.astype(F32)
        line = jnp.sum(near * near + far * far, axis=0, keepdims=True)
        sums_ref[k ^ x] = line[:, :128] + line[:, 128:256] + line[:, 256:384] + line[:, 384:]
    weight_ref[:, :HALF] = left.astype(B16)
    weight_ref[:, HALF:] = right.astype(B16)
    total = sums_ref[0] + sums_ref[1] + sums_ref[2] + sums_ref[3]
    top = total.astype(B16).astype(F32)
    middle = (total - top).astype(B16).astype(F32)
    bottom = total - top - middle
    row = lax.broadcasted_iota(jnp.int32, (16, 128), 0)
    lines = jnp.where(row == 0, top, jnp.where(row == 1, middle, jnp.where(row == 2, bottom, 0.0)))
    squares_ref[...] = lines.astype(B16)


def final_parts(place, gathered, student_out, heads):
    specs = [whole(256, HALF)] * 8 + [pl.BlockSpec((128, COLS), lambda i, m: (0, m[0])), whole(NX, 256, 128)]
    outs = [
        jax.ShapeDtypeStruct((NX, 256, 128), B16),
        jax.ShapeDtypeStruct((16, 128), B16),
        jax.ShapeDtypeStruct((128, COLS), B16),
    ]
    return call(final_kernel, specs, outs, 2 * 1024 * 1024 * 256, [pltpu.VMEM((NX, 1, 128), F32)])(
        place, *gathered, student_out, heads
    )


def local(
    teacher_heads,
    teacher_out,
    teacher_resid,
    matches,
    projector,
    student_heads,
    student_out,
    student_resid,
):
    seq = lax.axis_index("seq")
    member = lax.axis_index(COLUMN)
    place = jnp.stack([member, seq, lax.axis_index("x")]).astype(jnp.int32)
    swap = [(0, 1), (1, 0)]

    there = lax.ppermute(teacher_heads, "seq", swap)
    first, held = own_parts(place, teacher_heads, teacher_out)
    second = there_parts(place, there, held)

    second[2], later = lax.optimization_barrier((second[2], member))
    away = lax.dynamic_slice(projector, (0, (later + 1 - 2 * seq) * COLS), (256, COLS))
    other = lax.ppermute(away, "seq", swap)

    summed, other = reduce_x(first, second, (away,), (other,))
    moved = lax.all_to_all(summed, "z", 0, 0)
    near = lax.dynamic_slice(teacher_resid, (seq * 64, 0), (64, 256))
    far = lax.dynamic_slice(teacher_resid, (64 - seq * 64, 0), (64, 256))
    hidden = (jnp.concatenate([near, far], axis=0).astype(F32) + jnp.sum(moved.astype(F32), axis=0)).astype(B16)

    spot, hidden = lax.optimization_barrier((place, hidden))
    weights, out_cols = layout(spot, projector, other, student_out)

    own_matches = lax.dynamic_slice(matches, (seq * 128,), (128,)).astype(B16)
    shared = jnp.concatenate(
        [hidden[:, :128], hidden[:, 128:], student_heads, jnp.broadcast_to(own_matches[None], (16, 128))], axis=0
    )
    resid_parts = jnp.transpose(student_resid.reshape(4, NY, 8, 128), (1, 0, 2, 3)).reshape(NY, 32, 128)
    sent = jnp.concatenate([jnp.broadcast_to(shared[None], (NY,) + shared.shape), resid_parts], axis=1)
    got = lax.all_to_all(sent, COLUMN, 0, 0)
    heads = own_order(got[:, 256:384]).reshape(NX, 256, 128)
    base = (jnp.arange(NY, dtype=jnp.int32) // 2 * 128)[:, None]
    picked = own_order(got[:, 384].astype(jnp.int32) + base).reshape(NX, 1, 256)
    operands = (place, picked, got, heads, out_cols, weights)
    far = [part.reshape(NZ, 32, HALF) for part in combined_parts(FAR, *operands)]
    rest = [part.reshape(NZ, 32, HALF) for part in combined_parts(REST, *operands)]
    resid = got[:, 400:].reshape(32, 2, HALF)
    resid = jnp.concatenate([resid[:, 0], resid[:, 1]], axis=0)
    (summed,) = reduce_x((rest[2], rest[0], far[0], rest[1]), (rest[5], rest[3], far[1], rest[4]), ())
    summed = reduce_z(summed)
    difference = resid.astype(F32) + summed
    grad = (difference * 0.125).astype(B16)

    tall = lax.all_to_all(jnp.broadcast_to(grad[None], (NZ, 64, HALF)), "z", 0, 0)
    gathered = gather_x(tall[:, :32].reshape(256, HALF), tall[:, 32:].reshape(256, HALF))

    heads_part, squares, grad_weight = final_parts(place, gathered, student_out, heads)
    sent = jnp.concatenate(
        [block_order(heads_part.reshape(ROWS, 128)), jnp.broadcast_to(squares[None], (NY, 16, 128))], axis=1
    )
    back = lax.all_to_all(sent, COLUMN, 0, 0).astype(F32)
    grad_heads = jnp.sum(back[:, :128], axis=0).astype(B16)
    total = jnp.sum(back[:, 128:])
    loss = (total * (64.0 / (ROWS * 8192))).reshape(1)
    return (loss, grad_heads, grad_weight)


def solution(mesh):
    cut = Mesh(mesh.devices.reshape(2, 2, 2, NZ, NX), COLUMN + PLANE)
    every = COLUMN + PLANE
    return jax.shard_map(
        local,
        mesh=cut,
        in_specs=(
            P(COLUMN, PLANE),
            P(PLANE, "seq"),
            P(GROUP, ("seq",) + PLANE),
            P(GROUP),
            P(("seq",) + PLANE, None),
            P(COLUMN, PLANE),
            P(PLANE, None),
            P(every, None),
        ),
        out_specs=(P(), P(COLUMN, PLANE), P(PLANE, COLUMN)),
        check_vma=False,
    )
```

```python
import functools

import jax
import jax.numpy as jnp
from jax import lax
from jax.experimental import pallas as pl
from jax.experimental.pallas import tpu as pltpu
from jax.sharding import Mesh, PartitionSpec as P

B16 = jnp.bfloat16
F32 = jnp.float32
NY, NZ, NX = 8, 8, 4
GROUP = ("ylo", "core")
COLUMN = ("ylo", "core", "seq")
PLANE = ("z", "x")
ROWS = 1024
COLS = 1024
HALF = COLS // 2


def dot(a, b, dims):
    return lax.dot_general(a, b, (dims, ((), ())), preferred_element_type=F32)


def add(*terms):
    total = terms[0].astype(F32)
    for term in terms[1:]:
        total += term.astype(F32)
    return total.astype(B16)


def across(block, flip):
    return lax.ppermute(block, "x", [(i, i ^ flip) for i in range(NX)])


def reduce_x(first, second, before, tie=()):
    first_far = across(first[2], 1)
    second_far = across(second[2], 3)
    first_near, second_near, *before = lax.optimization_barrier((first[1], second[3], *before))
    first_near = across(first_near, 1)
    second_near = across(second_near, 3)
    first_last = across(add(first[3], first_far), 3)
    second_last = across(add(second[1], second_far), 1)
    if tie:
        second_last, *tie = lax.optimization_barrier((second_last, *tie))
    return (
        jnp.concatenate(
            [add(first[0], first_near, first_last), add(second[0], second_near, second_last)], axis=1
        ),
        *tie,
    )


def gather_x(first, second):
    first_three = across(first, 3)
    second_one = across(second, 1)
    first_one = across(first, 1)
    second_three = across(second, 3)
    first_two = across(first_three, 1)
    second_two = across(second_one, 3)
    return first, first_one, first_two, first_three, second, second_one, second_two, second_three


def reduce_z(parts):
    moved = lax.all_to_all(parts, "z", 0, 0)
    return jnp.sum(moved.astype(F32), axis=0)


def own_order(rows):
    rest = rows.shape[2:]
    parts = rows.reshape((NY, NZ, NX, 4) + rest)
    return jnp.transpose(parts, (2, 1, 0, 3) + tuple(range(4, parts.ndim))).reshape((ROWS,) + rest)


def block_order(rows):
    rest = rows.shape[1:]
    parts = rows.reshape((NX, NZ, NY, 4) + rest)
    return jnp.transpose(parts, (2, 1, 0, 3) + tuple(range(4, parts.ndim))).reshape((NY, 128) + rest)


def whole(*shape):
    return pl.BlockSpec(shape, lambda i, m: (0,) * len(shape))


def call(kernel, in_specs, outs, flops, scratch=(), limit=16):
    return pl.pallas_call(
        kernel,
        grid_spec=pltpu.PrefetchScalarGridSpec(
            num_scalar_prefetch=1,
            grid=(1,),
            in_specs=in_specs,
            out_specs=[whole(*out.shape) for out in outs],
            scratch_shapes=scratch,
        ),
        out_shape=outs,
        compiler_params=pltpu.CompilerParams(vmem_limit_bytes=limit << 20),
        cost_estimate=pl.CostEstimate(flops=flops, bytes_accessed=5 << 20, transcendentals=0),
    )


def load_kernel(place_ref, out_ref, held_ref, sems):
    copies = [
        pltpu.make_async_copy(out_ref.at[:, pl.ds(z * 1024, 1024)], held_ref.at[z], sems.at[z]) for z in range(NZ)
    ]
    for copy in copies:
        copy.start()
    for copy in copies:
        copy.wait()


def load(place, teacher_out):
    outs = [jax.ShapeDtypeStruct((NZ, 256, 1024), B16)]
    specs = [pl.BlockSpec(memory_space=pltpu.HBM)]
    return call(load_kernel, specs, outs, 1 << 21, [pltpu.SemaphoreType.DMA((NZ,))], 16)(place, teacher_out)[0]


def teacher_kernel(jobs, place_ref, own_ref, there_ref, held_ref, *parts):
    x = place_ref[2]
    rows = jnp.concatenate([own_ref[...], there_ref[...]], axis=0)
    for k, first, second in jobs:
        columns = pl.ds(pl.multiple_of((k ^ x) * 256, 256), 256)
        for z in range(NZ):
            product = dot(rows, held_ref[z, :, columns], ((1,), (0,))).astype(B16)
            parts[first][z] = product[:64]
            parts[second][z] = product[64:]


def teacher_parts(jobs, place, own, there, held):
    specs = [whole(64, 256), whole(64, 256), whole(NZ, 256, 1024)]
    outs = [jax.ShapeDtypeStruct((NZ, 64, 256), B16)] * (2 * len(jobs))
    flops = 2 * 128 * 256 * 2048 * len(jobs)
    return call(functools.partial(teacher_kernel, jobs), specs, outs, flops, (), 20)(place, own, there, held)


def layout_kernel(place_ref, home_in, other_in, out_in, weights_ref, out_ref):
    weights_ref[0:256, :] = home_in[...]
    weights_ref[256:512, :] = other_in[...]
    out_ref[...] = out_in[...]


def layout(place, projector, other, student_out):
    specs = [
        pl.BlockSpec((256, COLS), lambda i, m: (0, m[0])),
        whole(256, COLS),
        pl.BlockSpec((128, COLS), lambda i, m: (0, m[0])),
    ]
    outs = [jax.ShapeDtypeStruct((512, COLS), B16), jax.ShapeDtypeStruct((128, COLS), B16)]
    return call(layout_kernel, specs, outs, 1 << 21, (), 8)(place, projector, other, student_out)


def gather_hidden(place_ref, got_ref, hidden_ref):
    seq = place_ref[1]
    for g in range(4):
        near = pl.ds(pl.multiple_of(g * 128 + seq * 64, 64), 64)
        far = pl.ds(pl.multiple_of(g * 128 + 64 - seq * 64, 64), 64)
        for c in range(2):
            at, home, other = c * 128, slice(c * 128, c * 128 + 128), slice(256 + c * 128, 384 + c * 128)
            hidden_ref[near, home] = got_ref[2 * g + seq, at : at + 64, :]
            hidden_ref[far, home] = got_ref[2 * g + seq, at + 64 : at + 128, :]
            hidden_ref[far, other] = got_ref[2 * g + 1 - seq, at : at + 64, :]
            hidden_ref[near, other] = got_ref[2 * g + 1 - seq, at + 64 : at + 128, :]


def combine_kernel(jobs, place_ref, picked_ref, got_ref, heads_ref, out_ref, weights_ref, *refs):
    x = place_ref[2]
    parts, hidden_ref = refs[:-1], refs[-1]
    gather_hidden(place_ref, got_ref, hidden_ref)
    row = lax.broadcasted_iota(jnp.int32, (512, 256), 0)
    for k, halves in jobs:
        choose = (row == picked_ref[k ^ x]).astype(F32).astype(B16)
        selected = dot(choose, hidden_ref[...], ((0,), (0,))).astype(B16)
        heads = heads_ref[k ^ x]
        for half, to in halves:
            columns = slice(half * HALF, (half + 1) * HALF)
            total = dot(heads, out_ref[:, columns], ((1,), (0,)))
            total -= dot(selected, weights_ref[:, columns], ((1,), (0,)))
            parts[to][...] = total.astype(B16)


FAR = ((2, ((0, 0), (1, 1))),)
REST = ((1, ((0, 0), (1, 3))), (3, ((1, 4), (0, 1))), (0, ((0, 2), (1, 5))))


def combined_parts(jobs, place, picked, got, heads, out_cols, weights):
    specs = [whole(NX, 1, 256), whole(NY, 432, 128), whole(NX, 256, 128), whole(128, COLS), whole(512, COLS)]
    count = sum(len(halves) for _, halves in jobs)
    outs = [jax.ShapeDtypeStruct((256, HALF), B16)] * count
    return call(
        functools.partial(combine_kernel, jobs), specs, outs, count * 2 * 256 * 512 * 900, [pltpu.VMEM((512, 512), B16)], 16
    )(place, picked, got, heads, out_cols, weights)


def final_kernel(place_ref, *refs):
    x = place_ref[2]
    first, second = refs[:4], refs[4:8]
    out_ref, heads_ref, part_ref, squares_ref, weight_ref, sums_ref = refs[8:]
    left = jnp.zeros((128, HALF), F32)
    right = jnp.zeros((128, HALF), F32)
    for k in range(NX):
        near, far = first[k][...], second[k][...]
        part = dot(near, out_ref[:, :HALF], ((1,), (1,))) + dot(far, out_ref[:, HALF:], ((1,), (1,)))
        part_ref[k ^ x] = part.astype(B16)
        heads = heads_ref[k ^ x]
        left += dot(heads, near, ((0,), (0,)))
        right += dot(heads, far, ((0,), (0,)))
        near, far = near.astype(F32), far.astype(F32)
        line = jnp.sum(near * near + far * far, axis=0, keepdims=True)
        sums_ref[k ^ x] = line[:, :128] + line[:, 128:256] + line[:, 256:384] + line[:, 384:]
    weight_ref[:, :HALF] = left.astype(B16)
    weight_ref[:, HALF:] = right.astype(B16)
    total = sums_ref[0] + sums_ref[1] + sums_ref[2] + sums_ref[3]
    top = total.astype(B16).astype(F32)
    middle = (total - top).astype(B16).astype(F32)
    bottom = total - top - middle
    row = lax.broadcasted_iota(jnp.int32, (16, 128), 0)
    lines = jnp.where(row == 0, top, jnp.where(row == 1, middle, jnp.where(row == 2, bottom, 0.0)))
    squares_ref[...] = lines.astype(B16)


def final_parts(place, gathered, student_out, heads):
    specs = [whole(256, HALF)] * 8 + [pl.BlockSpec((128, COLS), lambda i, m: (0, m[0])), whole(NX, 256, 128)]
    outs = [
        jax.ShapeDtypeStruct((NX, 256, 128), B16),
        jax.ShapeDtypeStruct((16, 128), B16),
        jax.ShapeDtypeStruct((128, COLS), B16),
    ]
    return call(final_kernel, specs, outs, 2 * 1024 * 1024 * 256, [pltpu.VMEM((NX, 1, 128), F32)])(
        place, *gathered, student_out, heads
    )


def local(
    teacher_heads,
    teacher_out,
    teacher_resid,
    matches,
    projector,
    student_heads,
    student_out,
    student_resid,
):
    seq = lax.axis_index("seq")
    member = lax.axis_index(COLUMN)
    place = jnp.stack([member, seq, lax.axis_index("x")]).astype(jnp.int32)
    swap = [(0, 1), (1, 0)]

    there = lax.ppermute(teacher_heads, "seq", swap)
    held = load(place, teacher_out)
    far = teacher_parts(((2, 0, 1),), place, teacher_heads, there, held)
    rest = teacher_parts(((1, 0, 3), (3, 1, 4), (0, 2, 5)), place, teacher_heads, there, held)
    first = (rest[2], rest[0], far[0], rest[1])
    second = [rest[5], rest[3], far[1], rest[4]]

    second[2], later = lax.optimization_barrier((second[2], member))
    away = lax.dynamic_slice(projector, (0, (later + 1 - 2 * seq) * COLS), (256, COLS))
    other = lax.ppermute(away, "seq", swap)

    summed, other = reduce_x(first, second, (), (other,))
    moved = lax.all_to_all(summed, "z", 0, 0)
    near = lax.dynamic_slice(teacher_resid, (seq * 64, 0), (64, 256))
    far = lax.dynamic_slice(teacher_resid, (64 - seq * 64, 0), (64, 256))
    hidden = (jnp.concatenate([near, far], axis=0).astype(F32) + jnp.sum(moved.astype(F32), axis=0)).astype(B16)

    spot, hidden = lax.optimization_barrier((place, hidden))
    weights, out_cols = layout(spot, projector, other, student_out)

    own_matches = lax.dynamic_slice(matches, (seq * 128,), (128,)).astype(B16)
    shared = jnp.concatenate(
        [hidden[:, :128], hidden[:, 128:], student_heads, jnp.broadcast_to(own_matches[None], (16, 128))], axis=0
    )
    resid_parts = jnp.transpose(student_resid.reshape(4, NY, 8, 128), (1, 0, 2, 3)).reshape(NY, 32, 128)
    sent = jnp.concatenate([jnp.broadcast_to(shared[None], (NY,) + shared.shape), resid_parts], axis=1)
    got = lax.all_to_all(sent, COLUMN, 0, 0)
    heads = own_order(got[:, 256:384]).reshape(NX, 256, 128)
    base = (jnp.arange(NY, dtype=jnp.int32) // 2 * 128)[:, None]
    picked = own_order(got[:, 384].astype(jnp.int32) + base).reshape(NX, 1, 256)
    operands = (place, picked, got, heads, out_cols, weights)
    far = [part.reshape(NZ, 32, HALF) for part in combined_parts(FAR, *operands)]
    rest = [part.reshape(NZ, 32, HALF) for part in combined_parts(REST, *operands)]
    resid = got[:, 400:].reshape(32, 2, HALF)
    resid = jnp.concatenate([resid[:, 0], resid[:, 1]], axis=0)
    (summed,) = reduce_x((rest[2], rest[0], far[0], rest[1]), (rest[5], rest[3], far[1], rest[4]), ())
    summed = reduce_z(summed)
    difference = resid.astype(F32) + summed
    grad = (difference * 0.125).astype(B16)

    tall = lax.all_to_all(jnp.broadcast_to(grad[None], (NZ, 64, HALF)), "z", 0, 0)
    gathered = gather_x(tall[:, :32].reshape(256, HALF), tall[:, 32:].reshape(256, HALF))

    heads_part, squares, grad_weight = final_parts(place, gathered, student_out, heads)
    sent = jnp.concatenate(
        [block_order(heads_part.reshape(ROWS, 128)), jnp.broadcast_to(squares[None], (NY, 16, 128))], axis=1
    )
    back = lax.all_to_all(sent, COLUMN, 0, 0).astype(F32)
    grad_heads = jnp.sum(back[:, :128], axis=0).astype(B16)
    total = jnp.sum(back[:, 128:])
    loss = (total * (64.0 / (ROWS * 8192))).reshape(1)
    return (loss, grad_heads, grad_weight)


def solution(mesh):
    cut = Mesh(mesh.devices.reshape(2, 2, 2, NZ, NX), COLUMN + PLANE)
    every = COLUMN + PLANE
    return jax.shard_map(
        local,
        mesh=cut,
        in_specs=(
            P(COLUMN, PLANE),
            P(PLANE, "seq"),
            P(GROUP, ("seq",) + PLANE),
            P(GROUP),
            P(("seq",) + PLANE, None),
            P(COLUMN, PLANE),
            P(PLANE, None),
            P(every, None),
        ),
        out_specs=(P(), P(COLUMN, PLANE), P(PLANE, COLUMN)),
        check_vma=False,
    )
```

```python
import functools

import jax
import jax.numpy as jnp
from jax import lax
from jax.experimental import pallas as pl
from jax.experimental.pallas import tpu as pltpu
from jax.sharding import Mesh, PartitionSpec as P

B16 = jnp.bfloat16
F32 = jnp.float32
NY, NZ, NX = 8, 8, 4
GROUP = ("ylo", "core")
COLUMN = ("ylo", "core", "seq")
PLANE = ("z", "x")
ROWS = 1024
COLS = 1024
HALF = COLS // 2


def dot(a, b, dims):
    return lax.dot_general(a, b, (dims, ((), ())), preferred_element_type=F32)


def add(*terms):
    total = terms[0].astype(F32)
    for term in terms[1:]:
        total += term.astype(F32)
    return total.astype(B16)


def across(block, flip):
    return lax.ppermute(block, "x", [(i, i ^ flip) for i in range(NX)])


def reduce_x(first, second, before, tie=()):
    first_far = across(first[2], 1)
    second_far = across(second[2], 3)
    first_near, second_near, *before = lax.optimization_barrier((first[1], second[3], *before))
    first_near = across(first_near, 1)
    second_near = across(second_near, 3)
    first_last = across(add(first[3], first_far), 3)
    second_last = across(add(second[1], second_far), 1)
    if tie:
        second_last, *tie = lax.optimization_barrier((second_last, *tie))
    return (
        jnp.concatenate(
            [add(first[0], first_near, first_last), add(second[0], second_near, second_last)], axis=1
        ),
        *tie,
    )


def gather_x(first, second):
    first_three = across(first, 3)
    second_one = across(second, 1)
    first_one = across(first, 1)
    second_three = across(second, 3)
    first_two = across(first_three, 1)
    second_two = across(second_one, 3)
    return first, first_one, first_two, first_three, second, second_one, second_two, second_three


def reduce_z(parts):
    moved = lax.all_to_all(parts, "z", 0, 0)
    return jnp.sum(moved.astype(F32), axis=0)


def own_order(rows):
    rest = rows.shape[2:]
    parts = rows.reshape((NY, NZ, NX, 4) + rest)
    return jnp.transpose(parts, (2, 1, 0, 3) + tuple(range(4, parts.ndim))).reshape((ROWS,) + rest)


def block_order(rows):
    rest = rows.shape[1:]
    parts = rows.reshape((NX, NZ, NY, 4) + rest)
    return jnp.transpose(parts, (2, 1, 0, 3) + tuple(range(4, parts.ndim))).reshape((NY, 128) + rest)


def whole(*shape):
    return pl.BlockSpec(shape, lambda i, m: (0,) * len(shape))


def call(kernel, in_specs, outs, flops, scratch=(), limit=16):
    return pl.pallas_call(
        kernel,
        grid_spec=pltpu.PrefetchScalarGridSpec(
            num_scalar_prefetch=1,
            grid=(1,),
            in_specs=in_specs,
            out_specs=[whole(*out.shape) for out in outs],
            scratch_shapes=scratch,
        ),
        out_shape=outs,
        compiler_params=pltpu.CompilerParams(vmem_limit_bytes=limit << 20),
        cost_estimate=pl.CostEstimate(flops=flops, bytes_accessed=5 << 20, transcendentals=0),
    )


def load_kernel(place_ref, out_ref, held_ref, sems):
    copies = [
        pltpu.make_async_copy(out_ref.at[:, pl.ds(z * 1024, 1024)], held_ref.at[z], sems.at[z]) for z in range(NZ)
    ]
    for copy in copies:
        copy.start()
    for copy in copies:
        copy.wait()


def load(place, teacher_out):
    outs = [jax.ShapeDtypeStruct((NZ, 256, 1024), B16)]
    specs = [pl.BlockSpec(memory_space=pltpu.HBM)]
    return call(load_kernel, specs, outs, 1 << 21, [pltpu.SemaphoreType.DMA((NZ,))], 16)(place, teacher_out)[0]


def teacher_kernel(jobs, place_ref, own_ref, there_ref, held_ref, *parts):
    x = place_ref[2]
    rows = jnp.concatenate([own_ref[...], there_ref[...]], axis=0)
    for k, first, second in jobs:
        columns = pl.ds(pl.multiple_of((k ^ x) * 256, 256), 256)
        for z in range(NZ):
            product = dot(rows, held_ref[z, :, columns], ((1,), (0,))).astype(B16)
            parts[first][z] = product[:64]
            parts[second][z] = product[64:]


def teacher_parts(jobs, place, own, there, held):
    specs = [whole(64, 256), whole(64, 256), whole(NZ, 256, 1024)]
    outs = [jax.ShapeDtypeStruct((NZ, 64, 256), B16)] * (2 * len(jobs))
    flops = 2 * 128 * 256 * 2048 * len(jobs)
    return call(functools.partial(teacher_kernel, jobs), specs, outs, flops, (), 20)(place, own, there, held)


def payload_kernel(place_ref, moved_ref, resid_ref, heads_ref, matches_ref, parts_ref, sent_ref):
    seq = place_ref[1]
    summed = moved_ref[0].astype(F32)
    for z in range(1, NZ):
        summed += moved_ref[z].astype(F32)
    near = resid_ref[pl.ds(pl.multiple_of(seq * 64, 64), 64), :]
    far = resid_ref[pl.ds(pl.multiple_of(64 - seq * 64, 64), 64), :]
    hidden = (jnp.concatenate([near, far], axis=0).astype(F32) + summed).astype(B16)
    matched = jnp.broadcast_to(matches_ref[...].astype(F32), (16, 128)).astype(B16)
    for gs in range(NY):
        sent_ref[gs, 0:128, :] = hidden[:, :128]
        sent_ref[gs, 128:256, :] = hidden[:, 128:]
        sent_ref[gs, 256:384, :] = heads_ref[...]
        sent_ref[gs, 384:400, :] = matched
        sent_ref[gs, 400:432, :] = parts_ref[gs]


def payload(place, moved, resid, heads, matches, parts):
    specs = [whole(NZ, 128, 256), whole(128, 256), whole(128, 128), whole(1, 128), whole(NY, 32, 128)]
    outs = [jax.ShapeDtypeStruct((NY, 432, 128), B16)]
    return call(payload_kernel, specs, outs, 1 << 20)(place, moved, resid, heads, matches, parts)[0]


def last_kernel(place_ref, back_ref, grad_ref, lines_ref):
    grad = back_ref[0, 0:128, :].astype(F32)
    lines = back_ref[0, 128:144, :].astype(F32)
    for gs in range(1, NY):
        grad += back_ref[gs, 0:128, :].astype(F32)
        lines += back_ref[gs, 128:144, :].astype(F32)
    grad_ref[...] = grad.astype(B16)
    total = jnp.sum(jnp.sum(lines, axis=1, keepdims=True), axis=0, keepdims=True)
    lines_ref[...] = jnp.broadcast_to(total * (64.0 / (ROWS * 8192)), (1, 128))


def last_sums(place, back):
    outs = [jax.ShapeDtypeStruct((128, 128), B16), jax.ShapeDtypeStruct((1, 128), F32)]
    return call(last_kernel, [whole(NY, 144, 128)], outs, 1 << 18)(place, back)


def layout_kernel(place_ref, home_in, other_in, out_in, weights_ref, out_ref):
    weights_ref[0:256, :] = home_in[...]
    weights_ref[256:512, :] = other_in[...]
    out_ref[...] = out_in[...]


def layout(place, projector, other, student_out):
    specs = [
        pl.BlockSpec((256, COLS), lambda i, m: (0, m[0])),
        whole(256, COLS),
        pl.BlockSpec((128, COLS), lambda i, m: (0, m[0])),
    ]
    outs = [jax.ShapeDtypeStruct((512, COLS), B16), jax.ShapeDtypeStruct((128, COLS), B16)]
    return call(layout_kernel, specs, outs, 1 << 21, (), 8)(place, projector, other, student_out)


def gather_hidden(place_ref, got_ref, hidden_ref):
    seq = place_ref[1]
    for g in range(4):
        near = pl.ds(pl.multiple_of(g * 128 + seq * 64, 64), 64)
        far = pl.ds(pl.multiple_of(g * 128 + 64 - seq * 64, 64), 64)
        for c in range(2):
            at, home, other = c * 128, slice(c * 128, c * 128 + 128), slice(256 + c * 128, 384 + c * 128)
            hidden_ref[near, home] = got_ref[2 * g + seq, at : at + 64, :]
            hidden_ref[far, home] = got_ref[2 * g + seq, at + 64 : at + 128, :]
            hidden_ref[far, other] = got_ref[2 * g + 1 - seq, at : at + 64, :]
            hidden_ref[near, other] = got_ref[2 * g + 1 - seq, at + 64 : at + 128, :]


def combine_kernel(jobs, place_ref, picked_ref, got_ref, heads_ref, out_ref, weights_ref, *refs):
    x = place_ref[2]
    parts, hidden_ref = refs[:-1], refs[-1]
    gather_hidden(place_ref, got_ref, hidden_ref)
    row = lax.broadcasted_iota(jnp.int32, (512, 256), 0)
    for k, halves in jobs:
        choose = (row == picked_ref[k ^ x]).astype(F32).astype(B16)
        selected = dot(choose, hidden_ref[...], ((0,), (0,))).astype(B16)
        heads = heads_ref[k ^ x]
        for half, to in halves:
            columns = slice(half * HALF, (half + 1) * HALF)
            total = dot(heads, out_ref[:, columns], ((1,), (0,)))
            total -= dot(selected, weights_ref[:, columns], ((1,), (0,)))
            parts[to][...] = total.astype(B16)


FAR = ((2, ((0, 0), (1, 1))),)
REST = ((1, ((0, 0), (1, 3))), (3, ((1, 4), (0, 1))), (0, ((0, 2), (1, 5))))


def combined_parts(jobs, place, picked, got, heads, out_cols, weights):
    specs = [whole(NX, 1, 256), whole(NY, 432, 128), whole(NX, 256, 128), whole(128, COLS), whole(512, COLS)]
    count = sum(len(halves) for _, halves in jobs)
    outs = [jax.ShapeDtypeStruct((256, HALF), B16)] * count
    return call(
        functools.partial(combine_kernel, jobs), specs, outs, count * 2 * 256 * 512 * 900, [pltpu.VMEM((512, 512), B16)], 16
    )(place, picked, got, heads, out_cols, weights)


def final_kernel(place_ref, *refs):
    x = place_ref[2]
    first, second = refs[:4], refs[4:8]
    out_ref, heads_ref, part_ref, squares_ref, weight_ref, sums_ref = refs[8:]
    left = jnp.zeros((128, HALF), F32)
    right = jnp.zeros((128, HALF), F32)
    for k in range(NX):
        near, far = first[k][...], second[k][...]
        part = dot(near, out_ref[:, :HALF], ((1,), (1,))) + dot(far, out_ref[:, HALF:], ((1,), (1,)))
        part_ref[k ^ x] = part.astype(B16)
        heads = heads_ref[k ^ x]
        left += dot(heads, near, ((0,), (0,)))
        right += dot(heads, far, ((0,), (0,)))
        near, far = near.astype(F32), far.astype(F32)
        line = jnp.sum(near * near + far * far, axis=0, keepdims=True)
        sums_ref[k ^ x] = line[:, :128] + line[:, 128:256] + line[:, 256:384] + line[:, 384:]
    weight_ref[:, :HALF] = left.astype(B16)
    weight_ref[:, HALF:] = right.astype(B16)
    total = sums_ref[0] + sums_ref[1] + sums_ref[2] + sums_ref[3]
    top = total.astype(B16).astype(F32)
    middle = (total - top).astype(B16).astype(F32)
    bottom = total - top - middle
    row = lax.broadcasted_iota(jnp.int32, (16, 128), 0)
    lines = jnp.where(row == 0, top, jnp.where(row == 1, middle, jnp.where(row == 2, bottom, 0.0)))
    squares_ref[...] = lines.astype(B16)


def final_parts(place, gathered, student_out, heads):
    specs = [whole(256, HALF)] * 8 + [pl.BlockSpec((128, COLS), lambda i, m: (0, m[0])), whole(NX, 256, 128)]
    outs = [
        jax.ShapeDtypeStruct((NX, 256, 128), B16),
        jax.ShapeDtypeStruct((16, 128), B16),
        jax.ShapeDtypeStruct((128, COLS), B16),
    ]
    return call(final_kernel, specs, outs, 2 * 1024 * 1024 * 256, [pltpu.VMEM((NX, 1, 128), F32)])(
        place, *gathered, student_out, heads
    )


def local(
    teacher_heads,
    teacher_out,
    teacher_resid,
    matches,
    projector,
    student_heads,
    student_out,
    student_resid,
):
    seq = lax.axis_index("seq")
    member = lax.axis_index(COLUMN)
    place = jnp.stack([member, seq, lax.axis_index("x")]).astype(jnp.int32)
    swap = [(0, 1), (1, 0)]

    there = lax.ppermute(teacher_heads, "seq", swap)
    held = load(place, teacher_out)
    jobs = ((2, 2, 6), (1, 1, 5), (3, 3, 7), (0, 0, 4))
    parts = list(teacher_parts(jobs, place, teacher_heads, there, held))
    first, second = parts[:NX], parts[NX:]

    second[0], later = lax.optimization_barrier((second[0], member))
    away = lax.dynamic_slice(projector, (0, (later + 1 - 2 * seq) * COLS), (256, COLS))
    other = lax.ppermute(away, "seq", swap)

    summed, other = reduce_x(first, second, (away,), (other,))
    moved = lax.all_to_all(summed, "z", 0, 0)
    own_matches = lax.dynamic_slice(matches, (seq * 128,), (128,)).astype(B16)
    resid_parts = jnp.transpose(student_resid.reshape(4, NY, 8, 128), (1, 0, 2, 3)).reshape(NY, 32, 128)
    sent = payload(place, moved, teacher_resid, student_heads, own_matches.reshape(1, 128), resid_parts)
    spot, sent = lax.optimization_barrier((place, sent))
    weights, out_cols = layout(spot, projector, other, student_out)
    got = lax.all_to_all(sent, COLUMN, 0, 0)
    heads = own_order(got[:, 256:384]).reshape(NX, 256, 128)
    base = (jnp.arange(NY, dtype=jnp.int32) // 2 * 128)[:, None]
    picked = own_order(got[:, 384].astype(jnp.int32) + base).reshape(NX, 1, 256)
    operands = (place, picked, got, heads, out_cols, weights)
    far = [part.reshape(NZ, 32, HALF) for part in combined_parts(FAR, *operands)]
    rest = [part.reshape(NZ, 32, HALF) for part in combined_parts(REST, *operands)]
    resid = got[:, 400:].reshape(32, 2, HALF)
    resid = jnp.concatenate([resid[:, 0], resid[:, 1]], axis=0)
    (summed,) = reduce_x((rest[2], rest[0], far[0], rest[1]), (rest[5], rest[3], far[1], rest[4]), ())
    summed = reduce_z(summed)
    difference = resid.astype(F32) + summed
    grad = (difference * 0.125).astype(B16)

    tall = lax.all_to_all(jnp.broadcast_to(grad[None], (NZ, 64, HALF)), "z", 0, 0)
    gathered = gather_x(tall[:, :32].reshape(256, HALF), tall[:, 32:].reshape(256, HALF))

    heads_part, squares, grad_weight = final_parts(place, gathered, student_out, heads)
    sent = jnp.concatenate(
        [block_order(heads_part.reshape(ROWS, 128)), jnp.broadcast_to(squares[None], (NY, 16, 128))], axis=1
    )
    back = lax.all_to_all(sent, COLUMN, 0, 0)
    grad_heads, loss = last_sums(place, back)
    loss = loss[0, :1]
    return (loss, grad_heads, grad_weight)


def solution(mesh):
    cut = Mesh(mesh.devices.reshape(2, 2, 2, NZ, NX), COLUMN + PLANE)
    every = COLUMN + PLANE
    return jax.shard_map(
        local,
        mesh=cut,
        in_specs=(
            P(COLUMN, PLANE),
            P(PLANE, "seq"),
            P(GROUP, ("seq",) + PLANE),
            P(GROUP),
            P(("seq",) + PLANE, None),
            P(COLUMN, PLANE),
            P(PLANE, None),
            P(every, None),
        ),
        out_specs=(P(), P(COLUMN, PLANE), P(PLANE, COLUMN)),
        check_vma=False,
    )
```

```python
import functools

import jax
import jax.numpy as jnp
from jax import lax
from jax.experimental import pallas as pl
from jax.experimental.pallas import tpu as pltpu
from jax.sharding import Mesh, PartitionSpec as P

B16 = jnp.bfloat16
F32 = jnp.float32
NY, NZ, NX = 8, 8, 4
GROUP = ("ylo", "core")
COLUMN = ("ylo", "core", "seq")
PLANE = ("z", "x")
ROWS = 1024
COLS = 1024
HALF = COLS // 2


def dot(a, b, dims):
    return lax.dot_general(a, b, (dims, ((), ())), preferred_element_type=F32)


def add(*terms):
    total = terms[0].astype(F32)
    for term in terms[1:]:
        total += term.astype(F32)
    return total.astype(B16)


def across(block, flip):
    return lax.ppermute(block, "x", [(i, i ^ flip) for i in range(NX)])


def reduce_x(first, second, before, tie=()):
    first_far = across(first[2], 1)
    second_far = across(second[2], 3)
    first_near, second_near, *before = lax.optimization_barrier((first[1], second[3], *before))
    first_near = across(first_near, 1)
    second_near = across(second_near, 3)
    first_last = across(add(first[3], first_far), 3)
    second_last = across(add(second[1], second_far), 1)
    if tie:
        second_last, *tie = lax.optimization_barrier((second_last, *tie))
    return (
        jnp.concatenate(
            [add(first[0], first_near, first_last), add(second[0], second_near, second_last)], axis=1
        ),
        *tie,
    )


def gather_x(first, second):
    first_three = across(first, 3)
    second_one = across(second, 1)
    first_one = across(first, 1)
    second_three = across(second, 3)
    first_two = across(first_three, 1)
    second_two = across(second_one, 3)
    return first, first_one, first_two, first_three, second, second_one, second_two, second_three


def own_order(rows):
    rest = rows.shape[2:]
    parts = rows.reshape((NY, NZ, NX, 4) + rest)
    return jnp.transpose(parts, (2, 1, 0, 3) + tuple(range(4, parts.ndim))).reshape((ROWS,) + rest)


def block_order(rows):
    rest = rows.shape[1:]
    parts = rows.reshape((NX, NZ, NY, 4) + rest)
    return jnp.transpose(parts, (2, 1, 0, 3) + tuple(range(4, parts.ndim))).reshape((NY, 128) + rest)


def whole(*shape):
    return pl.BlockSpec(shape, lambda i, m: (0,) * len(shape))


def call(kernel, in_specs, outs, flops, scratch=(), limit=16):
    return pl.pallas_call(
        kernel,
        grid_spec=pltpu.PrefetchScalarGridSpec(
            num_scalar_prefetch=1,
            grid=(1,),
            in_specs=in_specs,
            out_specs=[whole(*out.shape) for out in outs],
            scratch_shapes=scratch,
        ),
        out_shape=outs,
        compiler_params=pltpu.CompilerParams(vmem_limit_bytes=limit << 20),
        cost_estimate=pl.CostEstimate(flops=flops, bytes_accessed=5 << 20, transcendentals=0),
    )


def load_kernel(place_ref, out_ref, held_ref, sems):
    copies = [
        pltpu.make_async_copy(out_ref.at[:, pl.ds(z * 1024, 1024)], held_ref.at[z], sems.at[z]) for z in range(NZ)
    ]
    for copy in copies:
        copy.start()
    for copy in copies:
        copy.wait()


def load(place, teacher_out):
    outs = [jax.ShapeDtypeStruct((NZ, 256, 1024), B16)]
    specs = [pl.BlockSpec(memory_space=pltpu.HBM)]
    return call(load_kernel, specs, outs, 1 << 21, [pltpu.SemaphoreType.DMA((NZ,))], 16)(place, teacher_out)[0]


def teacher_kernel(jobs, place_ref, own_ref, there_ref, held_ref, *parts):
    x = place_ref[2]
    rows = jnp.concatenate([own_ref[...], there_ref[...]], axis=0)
    for k, first, second in jobs:
        columns = pl.ds(pl.multiple_of((k ^ x) * 256, 256), 256)
        for z in range(NZ):
            product = dot(rows, held_ref[z, :, columns], ((1,), (0,))).astype(B16)
            parts[first][z] = product[:64]
            parts[second][z] = product[64:]


def teacher_parts(jobs, place, own, there, held):
    specs = [whole(64, 256), whole(64, 256), whole(NZ, 256, 1024)]
    outs = [jax.ShapeDtypeStruct((NZ, 64, 256), B16)] * (2 * len(jobs))
    flops = 2 * 128 * 256 * 2048 * len(jobs)
    return call(functools.partial(teacher_kernel, jobs), specs, outs, flops, (), 20)(place, own, there, held)


def payload_kernel(place_ref, moved_ref, resid_ref, heads_ref, matches_ref, parts_ref, sent_ref):
    seq = place_ref[1]
    summed = moved_ref[0].astype(F32)
    for z in range(1, NZ):
        summed += moved_ref[z].astype(F32)
    near = resid_ref[pl.ds(pl.multiple_of(seq * 64, 64), 64), :]
    far = resid_ref[pl.ds(pl.multiple_of(64 - seq * 64, 64), 64), :]
    hidden = (jnp.concatenate([near, far], axis=0).astype(F32) + summed).astype(B16)
    matched = jnp.broadcast_to(matches_ref[...].astype(F32), (16, 128)).astype(B16)
    for gs in range(NY):
        sent_ref[gs, 0:128, :] = hidden[:, :128]
        sent_ref[gs, 128:256, :] = hidden[:, 128:]
        sent_ref[gs, 256:384, :] = heads_ref[...]
        sent_ref[gs, 384:400, :] = matched
        sent_ref[gs, 400:432, :] = parts_ref[gs]


def payload(place, moved, resid, heads, matches, parts):
    specs = [whole(NZ, 128, 256), whole(128, 256), whole(128, 128), whole(1, 128), whole(NY, 32, 128)]
    outs = [jax.ShapeDtypeStruct((NY, 432, 128), B16)]
    return call(payload_kernel, specs, outs, 1 << 20)(place, moved, resid, heads, matches, parts)[0]


def gradient_kernel(place_ref, moved_ref, resid_ref, grad_ref):
    total = moved_ref[0].astype(F32)
    for z in range(1, NZ):
        total += moved_ref[z].astype(F32)
    grad = ((resid_ref[...].astype(F32) + total) * 0.125).astype(B16)
    for z in range(NZ):
        grad_ref[z] = grad


def gradient_piece(place, moved, resid):
    outs = [jax.ShapeDtypeStruct((NZ, 64, HALF), B16)]
    specs = [whole(NZ, 64, HALF), whole(64, HALF)]
    return call(gradient_kernel, specs, outs, 1 << 19, (), 8)(place, moved, resid)[0]


def last_kernel(place_ref, back_ref, grad_ref, lines_ref):
    grad = back_ref[0, 0:128, :].astype(F32)
    lines = back_ref[0, 128:144, :].astype(F32)
    for gs in range(1, NY):
        grad += back_ref[gs, 0:128, :].astype(F32)
        lines += back_ref[gs, 128:144, :].astype(F32)
    grad_ref[...] = grad.astype(B16)
    total = jnp.sum(jnp.sum(lines, axis=1, keepdims=True), axis=0, keepdims=True)
    lines_ref[...] = jnp.broadcast_to(total * (64.0 / (ROWS * 8192)), (1, 128))


def last_sums(place, back):
    outs = [jax.ShapeDtypeStruct((128, 128), B16), jax.ShapeDtypeStruct((1, 128), F32)]
    return call(last_kernel, [whole(NY, 144, 128)], outs, 1 << 18)(place, back)


def layout_kernel(place_ref, home_in, other_in, out_in, weights_ref):
    weights_ref[0:256, :] = home_in[...]
    weights_ref[256:512, :] = other_in[...]
    weights_ref[512:640, :] = out_in[...]


def layout(place, projector, other, student_out):
    specs = [
        pl.BlockSpec((256, COLS), lambda i, m: (0, m[0])),
        whole(256, COLS),
        pl.BlockSpec((128, COLS), lambda i, m: (0, m[0])),
    ]
    outs = [jax.ShapeDtypeStruct((640, COLS), B16)]
    return call(layout_kernel, specs, outs, 1 << 21, (), 8)(place, projector, other, student_out)[0]


def gather_hidden(place_ref, got_ref, hidden_ref):
    seq = place_ref[1]
    for g in range(4):
        near = pl.ds(pl.multiple_of(g * 128 + seq * 64, 64), 64)
        far = pl.ds(pl.multiple_of(g * 128 + 64 - seq * 64, 64), 64)
        for c in range(2):
            at, home, other = c * 128, slice(c * 128, c * 128 + 128), slice(256 + c * 128, 384 + c * 128)
            hidden_ref[near, home] = got_ref[2 * g + seq, at : at + 64, :]
            hidden_ref[far, home] = got_ref[2 * g + seq, at + 64 : at + 128, :]
            hidden_ref[far, other] = got_ref[2 * g + 1 - seq, at : at + 64, :]
            hidden_ref[near, other] = got_ref[2 * g + 1 - seq, at + 64 : at + 128, :]


def combine_kernel(jobs, place_ref, picked_ref, got_ref, heads_ref, weights_ref, *refs):
    x = place_ref[2]
    parts, hidden_ref = refs[:-1], refs[-1]
    gather_hidden(place_ref, got_ref, hidden_ref)
    row = lax.broadcasted_iota(jnp.int32, (512, 256), 0)
    for k, halves in jobs:
        choose = (row == picked_ref[k ^ x]).astype(F32).astype(B16)
        selected = dot(choose, hidden_ref[...], ((0,), (0,))).astype(B16)
        heads = heads_ref[k ^ x]
        for half, to in halves:
            columns = slice(half * HALF, (half + 1) * HALF)
            total = dot(heads, weights_ref[512:640, columns], ((1,), (0,)))
            total -= dot(selected, weights_ref[0:512, columns], ((1,), (0,)))
            parts[to][...] = total.astype(B16)


FAR = ((2, ((0, 0), (1, 1))),)
REST = ((1, ((0, 0), (1, 3))), (3, ((1, 4), (0, 1))), (0, ((0, 2), (1, 5))))


def combined_parts(jobs, place, picked, got, heads, weights):
    specs = [whole(NX, 1, 256), whole(NY, 432, 128), whole(NX, 256, 128), whole(640, COLS)]
    count = sum(len(halves) for _, halves in jobs)
    outs = [jax.ShapeDtypeStruct((256, HALF), B16)] * count
    return call(
        functools.partial(combine_kernel, jobs), specs, outs, count * 2 * 256 * 512 * 900, [pltpu.VMEM((512, 512), B16)], 16
    )(place, picked, got, heads, weights)


def final_kernel(place_ref, *refs):
    x = place_ref[2]
    first, second = refs[:4], refs[4:8]
    out_ref, heads_ref, part_ref, squares_ref, weight_ref, sums_ref = refs[8:]
    left = jnp.zeros((128, HALF), F32)
    right = jnp.zeros((128, HALF), F32)
    for k in range(NX):
        near, far = first[k][...], second[k][...]
        part = dot(near, out_ref[:, :HALF], ((1,), (1,))) + dot(far, out_ref[:, HALF:], ((1,), (1,)))
        part_ref[k ^ x] = part.astype(B16)
        heads = heads_ref[k ^ x]
        left += dot(heads, near, ((0,), (0,)))
        right += dot(heads, far, ((0,), (0,)))
        near, far = near.astype(F32), far.astype(F32)
        line = jnp.sum(near * near + far * far, axis=0, keepdims=True)
        sums_ref[k ^ x] = line[:, :128] + line[:, 128:256] + line[:, 256:384] + line[:, 384:]
    weight_ref[:, :HALF] = left.astype(B16)
    weight_ref[:, HALF:] = right.astype(B16)
    total = sums_ref[0] + sums_ref[1] + sums_ref[2] + sums_ref[3]
    top = total.astype(B16).astype(F32)
    middle = (total - top).astype(B16).astype(F32)
    bottom = total - top - middle
    row = lax.broadcasted_iota(jnp.int32, (16, 128), 0)
    lines = jnp.where(row == 0, top, jnp.where(row == 1, middle, jnp.where(row == 2, bottom, 0.0)))
    squares_ref[...] = lines.astype(B16)


def final_parts(place, gathered, student_out, heads):
    specs = [whole(256, HALF)] * 8 + [pl.BlockSpec((128, COLS), lambda i, m: (0, m[0])), whole(NX, 256, 128)]
    outs = [
        jax.ShapeDtypeStruct((NX, 256, 128), B16),
        jax.ShapeDtypeStruct((16, 128), B16),
        jax.ShapeDtypeStruct((128, COLS), B16),
    ]
    return call(final_kernel, specs, outs, 2 * 1024 * 1024 * 256, [pltpu.VMEM((NX, 1, 128), F32)])(
        place, *gathered, student_out, heads
    )


def local(
    teacher_heads,
    teacher_out,
    teacher_resid,
    matches,
    projector,
    student_heads,
    student_out,
    student_resid,
):
    seq = lax.axis_index("seq")
    member = lax.axis_index(COLUMN)
    place = jnp.stack([member, seq, lax.axis_index("x")]).astype(jnp.int32)
    swap = [(0, 1), (1, 0)]

    there = lax.ppermute(teacher_heads, "seq", swap)
    held = load(place, teacher_out)
    jobs = ((2, 2, 6), (1, 1, 5), (3, 3, 7), (0, 0, 4))
    parts = list(teacher_parts(jobs, place, teacher_heads, there, held))
    first, second = parts[:NX], parts[NX:]

    second[0], later = lax.optimization_barrier((second[0], member))
    away = lax.dynamic_slice(projector, (0, (later + 1 - 2 * seq) * COLS), (256, COLS))
    other = lax.ppermute(away, "seq", swap)

    summed, other = reduce_x(first, second, (away,), (other,))
    moved = lax.all_to_all(summed, "z", 0, 0)
    own_matches = lax.dynamic_slice(matches, (seq * 128,), (128,)).astype(B16)
    resid_parts = jnp.transpose(student_resid.reshape(4, NY, 8, 128), (1, 0, 2, 3)).reshape(NY, 32, 128)
    sent = payload(place, moved, teacher_resid, student_heads, own_matches.reshape(1, 128), resid_parts)
    spot, sent = lax.optimization_barrier((place, sent))
    weights = layout(spot, projector, other, student_out)
    got = lax.all_to_all(sent, COLUMN, 0, 0)
    heads = own_order(got[:, 256:384]).reshape(NX, 256, 128)
    base = (jnp.arange(NY, dtype=jnp.int32) // 2 * 128)[:, None]
    picked = own_order(got[:, 384].astype(jnp.int32) + base).reshape(NX, 1, 256)
    operands = (place, picked, got, heads, weights)
    far = [part.reshape(NZ, 32, HALF) for part in combined_parts(FAR, *operands)]
    rest = [part.reshape(NZ, 32, HALF) for part in combined_parts(REST, *operands)]
    resid = got[:, 400:].reshape(32, 2, HALF)
    resid = jnp.concatenate([resid[:, 0], resid[:, 1]], axis=0)
    (summed,) = reduce_x((rest[2], rest[0], far[0], rest[1]), (rest[5], rest[3], far[1], rest[4]), ())
    moved = lax.all_to_all(summed, "z", 0, 0)
    grad = gradient_piece(place, moved, resid)

    tall = lax.all_to_all(grad, "z", 0, 0)
    gathered = gather_x(tall[:, :32].reshape(256, HALF), tall[:, 32:].reshape(256, HALF))

    heads_part, squares, grad_weight = final_parts(place, gathered, student_out, heads)
    sent = jnp.concatenate(
        [block_order(heads_part.reshape(ROWS, 128)), jnp.broadcast_to(squares[None], (NY, 16, 128))], axis=1
    )
    back = lax.all_to_all(sent, COLUMN, 0, 0)
    grad_heads, loss = last_sums(place, back)
    loss = loss[0, :1]
    return (loss, grad_heads, grad_weight)


def solution(mesh):
    cut = Mesh(mesh.devices.reshape(2, 2, 2, NZ, NX), COLUMN + PLANE)
    every = COLUMN + PLANE
    return jax.shard_map(
        local,
        mesh=cut,
        in_specs=(
            P(COLUMN, PLANE),
            P(PLANE, "seq"),
            P(GROUP, ("seq",) + PLANE),
            P(GROUP),
            P(("seq",) + PLANE, None),
            P(COLUMN, PLANE),
            P(PLANE, None),
            P(every, None),
        ),
        out_specs=(P(), P(COLUMN, PLANE), P(PLANE, COLUMN)),
        check_vma=False,
    )
```

```python
import functools

import jax
import jax.numpy as jnp
from jax import lax
from jax.experimental import pallas as pl
from jax.experimental.pallas import tpu as pltpu
from jax.sharding import Mesh, PartitionSpec as P

B16 = jnp.bfloat16
F32 = jnp.float32
NY, NZ, NX = 8, 8, 4
GROUP = ("ylo", "core")
COLUMN = ("ylo", "core", "seq")
PLANE = ("z", "x")
ROWS = 1024
COLS = 1024
HALF = COLS // 2


def dot(a, b, dims):
    return lax.dot_general(a, b, (dims, ((), ())), preferred_element_type=F32)


def add(*terms):
    total = terms[0].astype(F32)
    for term in terms[1:]:
        total += term.astype(F32)
    return total.astype(B16)


def across(block, flip):
    return lax.ppermute(block, "x", [(i, i ^ flip) for i in range(NX)])


def reduce_x(first, second, before, tie=()):
    first_far = across(first[2], 1)
    second_far = across(second[2], 3)
    first_near, second_near, *before = lax.optimization_barrier((first[1], second[3], *before))
    first_near = across(first_near, 1)
    second_near = across(second_near, 3)
    first_last = across(add(first[3], first_far), 3)
    second_last = across(add(second[1], second_far), 1)
    if tie:
        second_last, *tie = lax.optimization_barrier((second_last, *tie))
    return (
        jnp.concatenate(
            [add(first[0], first_near, first_last), add(second[0], second_near, second_last)], axis=1
        ),
        *tie,
    )


def gather_x(first, second):
    first_three = across(first, 3)
    second_one = across(second, 1)
    first_one = across(first, 1)
    second_three = across(second, 3)
    first_two = across(first_three, 1)
    second_two = across(second_one, 3)
    return first, first_one, first_two, first_three, second, second_one, second_two, second_three


def own_order(rows):
    rest = rows.shape[2:]
    parts = rows.reshape((NY, NZ, NX, 4) + rest)
    return jnp.transpose(parts, (2, 1, 0, 3) + tuple(range(4, parts.ndim))).reshape((ROWS,) + rest)


def block_order(rows):
    rest = rows.shape[1:]
    parts = rows.reshape((NX, NZ, NY, 4) + rest)
    return jnp.transpose(parts, (2, 1, 0, 3) + tuple(range(4, parts.ndim))).reshape((NY, 128) + rest)


def whole(*shape):
    return pl.BlockSpec(shape, lambda i, m: (0,) * len(shape))


def call(kernel, in_specs, outs, flops, scratch=(), limit=16):
    return pl.pallas_call(
        kernel,
        grid_spec=pltpu.PrefetchScalarGridSpec(
            num_scalar_prefetch=1,
            grid=(1,),
            in_specs=in_specs,
            out_specs=[whole(*out.shape) for out in outs],
            scratch_shapes=scratch,
        ),
        out_shape=outs,
        compiler_params=pltpu.CompilerParams(vmem_limit_bytes=limit << 20),
        cost_estimate=pl.CostEstimate(flops=flops, bytes_accessed=5 << 20, transcendentals=0),
    )


def load_kernel(place_ref, out_ref, held_ref, sems):
    copies = [
        pltpu.make_async_copy(out_ref.at[:, pl.ds(z * 1024, 1024)], held_ref.at[z], sems.at[z]) for z in range(NZ)
    ]
    for copy in copies:
        copy.start()
    for copy in copies:
        copy.wait()


def load(place, teacher_out):
    outs = [jax.ShapeDtypeStruct((NZ, 256, 1024), B16)]
    specs = [pl.BlockSpec(memory_space=pltpu.HBM)]
    return call(load_kernel, specs, outs, 1 << 21, [pltpu.SemaphoreType.DMA((NZ,))], 16)(place, teacher_out)[0]


def teacher_kernel(jobs, place_ref, own_ref, there_ref, held_ref, *parts):
    x = place_ref[2]
    rows = jnp.concatenate([own_ref[...], there_ref[...]], axis=0)
    for k, first, second in jobs:
        columns = pl.ds(pl.multiple_of((k ^ x) * 256, 256), 256)
        for z in range(NZ):
            product = dot(rows, held_ref[z, :, columns], ((1,), (0,))).astype(B16)
            parts[first][z] = product[:64]
            parts[second][z] = product[64:]


def teacher_parts(jobs, place, own, there, held):
    specs = [whole(64, 256), whole(64, 256), whole(NZ, 256, 1024)]
    outs = [jax.ShapeDtypeStruct((NZ, 64, 256), B16)] * (2 * len(jobs))
    flops = 2 * 128 * 256 * 2048 * len(jobs)
    return call(functools.partial(teacher_kernel, jobs), specs, outs, flops, (), 20)(place, own, there, held)


def payload_kernel(place_ref, moved_ref, resid_ref, heads_ref, matches_ref, parts_ref, sent_ref):
    seq = place_ref[1]
    summed = moved_ref[0].astype(F32)
    for z in range(1, NZ):
        summed += moved_ref[z].astype(F32)
    near = resid_ref[pl.ds(pl.multiple_of(seq * 64, 64), 64), :]
    far = resid_ref[pl.ds(pl.multiple_of(64 - seq * 64, 64), 64), :]
    hidden = (jnp.concatenate([near, far], axis=0).astype(F32) + summed).astype(B16)
    matched = jnp.broadcast_to(matches_ref[...].astype(F32), (16, 128)).astype(B16)
    for gs in range(NY):
        sent_ref[gs, 0:128, :] = hidden[:, :128]
        sent_ref[gs, 128:256, :] = hidden[:, 128:]
        sent_ref[gs, 256:384, :] = heads_ref[...]
        sent_ref[gs, 384:400, :] = matched
        sent_ref[gs, 400:432, :] = parts_ref[gs]


def payload(place, moved, resid, heads, matches, parts):
    specs = [whole(NZ, 128, 256), whole(128, 256), whole(128, 128), whole(1, 128), whole(NY, 32, 128)]
    outs = [jax.ShapeDtypeStruct((NY, 432, 128), B16)]
    return call(payload_kernel, specs, outs, 1 << 20)(place, moved, resid, heads, matches, parts)[0]


def gradient_kernel(place_ref, moved_ref, resid_ref, grad_ref):
    total = moved_ref[0].astype(F32)
    for z in range(1, NZ):
        total += moved_ref[z].astype(F32)
    grad = ((resid_ref[...].astype(F32) + total) * 0.125).astype(B16)
    for z in range(NZ):
        grad_ref[z] = grad


def gradient_piece(place, moved, resid):
    outs = [jax.ShapeDtypeStruct((NZ, 64, HALF), B16)]
    specs = [whole(NZ, 64, HALF), whole(64, HALF)]
    return call(gradient_kernel, specs, outs, 1 << 19, (), 8)(place, moved, resid)[0]


def last_kernel(place_ref, back_ref, grad_ref, lines_ref):
    grad = back_ref[0, 0:128, :].astype(F32)
    lines = back_ref[0, 128:144, :].astype(F32)
    for gs in range(1, NY):
        grad += back_ref[gs, 0:128, :].astype(F32)
        lines += back_ref[gs, 128:144, :].astype(F32)
    grad_ref[...] = grad.astype(B16)
    total = jnp.sum(jnp.sum(lines, axis=1, keepdims=True), axis=0, keepdims=True)
    lines_ref[...] = jnp.broadcast_to(total * (64.0 / (ROWS * 8192)), (1, 128))


def last_sums(place, back):
    outs = [jax.ShapeDtypeStruct((128, 128), B16), jax.ShapeDtypeStruct((1, 128), F32)]
    return call(last_kernel, [whole(NY, 144, 128)], outs, 1 << 18)(place, back)


def layout_kernel(place_ref, home_in, other_in, weights_ref):
    weights_ref[0:256, :] = home_in[...]
    weights_ref[256:512, :] = other_in[...]


def layout(place, projector, other):
    specs = [pl.BlockSpec((256, COLS), lambda i, m: (0, m[0])), whole(256, COLS)]
    outs = [jax.ShapeDtypeStruct((512, COLS), B16)]
    return call(layout_kernel, specs, outs, 1 << 21, (), 8)(place, projector, other)[0]


def gather_hidden(place_ref, got_ref, hidden_ref):
    seq = place_ref[1]
    for g in range(4):
        near = pl.ds(pl.multiple_of(g * 128 + seq * 64, 64), 64)
        far = pl.ds(pl.multiple_of(g * 128 + 64 - seq * 64, 64), 64)
        for c in range(2):
            at, home, other = c * 128, slice(c * 128, c * 128 + 128), slice(256 + c * 128, 384 + c * 128)
            hidden_ref[near, home] = got_ref[2 * g + seq, at : at + 64, :]
            hidden_ref[far, home] = got_ref[2 * g + seq, at + 64 : at + 128, :]
            hidden_ref[far, other] = got_ref[2 * g + 1 - seq, at : at + 64, :]
            hidden_ref[near, other] = got_ref[2 * g + 1 - seq, at + 64 : at + 128, :]


def combine_kernel(jobs, place_ref, picked_ref, got_ref, heads_ref, out_ref, weights_ref, *refs):
    x = place_ref[2]
    parts, hidden_ref = refs[:-1], refs[-1]
    gather_hidden(place_ref, got_ref, hidden_ref)
    row = lax.broadcasted_iota(jnp.int32, (512, 256), 0)
    for k, halves in jobs:
        choose = (row == picked_ref[k ^ x]).astype(F32).astype(B16)
        selected = dot(choose, hidden_ref[...], ((0,), (0,))).astype(B16)
        heads = heads_ref[k ^ x]
        for half, to in halves:
            columns = slice(half * HALF, (half + 1) * HALF)
            total = dot(heads, out_ref[:, columns], ((1,), (0,)))
            total -= dot(selected, weights_ref[:, columns], ((1,), (0,)))
            parts[to][...] = total.astype(B16)


FAR = ((2, ((0, 0), (1, 1))),)
REST = ((1, ((0, 0), (1, 3))), (3, ((1, 4), (0, 1))), (0, ((0, 2), (1, 5))))


def combined_parts(jobs, place, picked, got, heads, student_out, weights):
    block = pl.BlockSpec((128, COLS), lambda i, m: (0, m[0]))
    specs = [whole(NX, 1, 256), whole(NY, 432, 128), whole(NX, 256, 128), block, whole(512, COLS)]
    count = sum(len(halves) for _, halves in jobs)
    outs = [jax.ShapeDtypeStruct((256, HALF), B16)] * count
    return call(
        functools.partial(combine_kernel, jobs), specs, outs, count * 2 * 256 * 512 * 900, [pltpu.VMEM((512, 512), B16)], 16
    )(place, picked, got, heads, student_out, weights)


def final_kernel(place_ref, *refs):
    x = place_ref[2]
    first, second = refs[:4], refs[4:8]
    out_ref, heads_ref, part_ref, squares_ref, weight_ref, sums_ref = refs[8:]
    left = jnp.zeros((128, HALF), F32)
    right = jnp.zeros((128, HALF), F32)
    for k in range(NX):
        near, far = first[k][...], second[k][...]
        part = dot(near, out_ref[:, :HALF], ((1,), (1,))) + dot(far, out_ref[:, HALF:], ((1,), (1,)))
        part_ref[k ^ x] = part.astype(B16)
        heads = heads_ref[k ^ x]
        left += dot(heads, near, ((0,), (0,)))
        right += dot(heads, far, ((0,), (0,)))
        near, far = near.astype(F32), far.astype(F32)
        line = jnp.sum(near * near + far * far, axis=0, keepdims=True)
        sums_ref[k ^ x] = line[:, :128] + line[:, 128:256] + line[:, 256:384] + line[:, 384:]
    weight_ref[:, :HALF] = left.astype(B16)
    weight_ref[:, HALF:] = right.astype(B16)
    total = sums_ref[0] + sums_ref[1] + sums_ref[2] + sums_ref[3]
    top = total.astype(B16).astype(F32)
    middle = (total - top).astype(B16).astype(F32)
    bottom = total - top - middle
    row = lax.broadcasted_iota(jnp.int32, (16, 128), 0)
    lines = jnp.where(row == 0, top, jnp.where(row == 1, middle, jnp.where(row == 2, bottom, 0.0)))
    squares_ref[...] = lines.astype(B16)


def final_parts(place, gathered, student_out, heads):
    specs = [whole(256, HALF)] * 8 + [pl.BlockSpec((128, COLS), lambda i, m: (0, m[0])), whole(NX, 256, 128)]
    outs = [
        jax.ShapeDtypeStruct((NX, 256, 128), B16),
        jax.ShapeDtypeStruct((16, 128), B16),
        jax.ShapeDtypeStruct((128, COLS), B16),
    ]
    return call(final_kernel, specs, outs, 2 * 1024 * 1024 * 256, [pltpu.VMEM((NX, 1, 128), F32)])(
        place, *gathered, student_out, heads
    )


def local(
    teacher_heads,
    teacher_out,
    teacher_resid,
    matches,
    projector,
    student_heads,
    student_out,
    student_resid,
):
    seq = lax.axis_index("seq")
    member = lax.axis_index(COLUMN)
    place = jnp.stack([member, seq, lax.axis_index("x")]).astype(jnp.int32)
    swap = [(0, 1), (1, 0)]

    there = lax.ppermute(teacher_heads, "seq", swap)
    held = load(place, teacher_out)
    jobs = ((2, 2, 6), (1, 1, 5), (3, 3, 7), (0, 0, 4))
    parts = list(teacher_parts(jobs, place, teacher_heads, there, held))
    first, second = parts[:NX], parts[NX:]

    second[0], later = lax.optimization_barrier((second[0], member))
    away = lax.dynamic_slice(projector, (0, (later + 1 - 2 * seq) * COLS), (256, COLS))
    other = lax.ppermute(away, "seq", swap)

    summed, other = reduce_x(first, second, (away,), (other,))
    moved = lax.all_to_all(summed, "z", 0, 0)
    own_matches = lax.dynamic_slice(matches, (seq * 128,), (128,)).astype(B16)
    resid_parts = jnp.transpose(student_resid.reshape(4, NY, 8, 128), (1, 0, 2, 3)).reshape(NY, 32, 128)
    sent = payload(place, moved, teacher_resid, student_heads, own_matches.reshape(1, 128), resid_parts)
    spot, sent = lax.optimization_barrier((place, sent))
    weights = layout(spot, projector, other)
    got = lax.all_to_all(sent, COLUMN, 0, 0)
    heads = own_order(got[:, 256:384]).reshape(NX, 256, 128)
    base = (jnp.arange(NY, dtype=jnp.int32) // 2 * 128)[:, None]
    picked = own_order(got[:, 384].astype(jnp.int32) + base).reshape(NX, 1, 256)
    operands = (place, picked, got, heads, student_out, weights)
    far = [part.reshape(NZ, 32, HALF) for part in combined_parts(FAR, *operands)]
    rest = [part.reshape(NZ, 32, HALF) for part in combined_parts(REST, *operands)]
    resid = got[:, 400:].reshape(32, 2, HALF)
    resid = jnp.concatenate([resid[:, 0], resid[:, 1]], axis=0)
    (summed,) = reduce_x((rest[2], rest[0], far[0], rest[1]), (rest[5], rest[3], far[1], rest[4]), ())
    moved = lax.all_to_all(summed, "z", 0, 0)
    grad = gradient_piece(place, moved, resid)

    tall = lax.all_to_all(grad, "z", 0, 0)
    gathered = gather_x(tall[:, :32].reshape(256, HALF), tall[:, 32:].reshape(256, HALF))

    heads_part, squares, grad_weight = final_parts(place, gathered, student_out, heads)
    sent = jnp.concatenate(
        [block_order(heads_part.reshape(ROWS, 128)), jnp.broadcast_to(squares[None], (NY, 16, 128))], axis=1
    )
    back = lax.all_to_all(sent, COLUMN, 0, 0)
    grad_heads, loss = last_sums(place, back)
    loss = loss[0, :1]
    return (loss, grad_heads, grad_weight)


def solution(mesh):
    cut = Mesh(mesh.devices.reshape(2, 2, 2, NZ, NX), COLUMN + PLANE)
    every = COLUMN + PLANE
    return jax.shard_map(
        local,
        mesh=cut,
        in_specs=(
            P(COLUMN, PLANE),
            P(PLANE, "seq"),
            P(GROUP, ("seq",) + PLANE),
            P(GROUP),
            P(("seq",) + PLANE, None),
            P(COLUMN, PLANE),
            P(PLANE, None),
            P(every, None),
        ),
        out_specs=(P(), P(COLUMN, PLANE), P(PLANE, COLUMN)),
        check_vma=False,
    )
```

```python
import functools

import jax
import jax.numpy as jnp
from jax import lax
from jax.experimental import pallas as pl
from jax.experimental.pallas import tpu as pltpu
from jax.sharding import Mesh, PartitionSpec as P

B16 = jnp.bfloat16
F32 = jnp.float32
NY, NZ, NX = 8, 8, 4
GROUP = ("ylo", "core")
COLUMN = ("ylo", "core", "seq")
PLANE = ("z", "x")
ROWS = 1024
COLS = 1024
HALF = COLS // 2


def dot(a, b, dims):
    return lax.dot_general(a, b, (dims, ((), ())), preferred_element_type=F32)


def add(*terms):
    total = terms[0].astype(F32)
    for term in terms[1:]:
        total += term.astype(F32)
    return total.astype(B16)


def across(block, flip):
    return lax.ppermute(block, "x", [(i, i ^ flip) for i in range(NX)])


def reduce_x(first, second, before, tie=()):
    first_far = across(first[2], 1)
    second_far = across(second[2], 3)
    first_near, second_near, *before = lax.optimization_barrier((first[1], second[3], *before))
    first_near = across(first_near, 1)
    second_near = across(second_near, 3)
    first_last = across(add(first[3], first_far), 3)
    second_last = across(add(second[1], second_far), 1)
    first_last, first_near, second_near = lax.optimization_barrier((first_last, first_near, second_near))
    if tie:
        second_last, *tie = lax.optimization_barrier((second_last, *tie))
    return (
        jnp.concatenate(
            [add(first[0], first_near, first_last), add(second[0], second_near, second_last)], axis=1
        ),
        *tie,
    )


def gather_x(first, second):
    first_three = across(first, 3)
    second_one = across(second, 1)
    first_one = across(first, 1)
    second_three = across(second, 3)
    first_two = across(first_three, 1)
    second_two = across(second_one, 3)
    return first, first_one, first_two, first_three, second, second_one, second_two, second_three


def own_order(rows):
    rest = rows.shape[2:]
    parts = rows.reshape((NY, NZ, NX, 4) + rest)
    return jnp.transpose(parts, (2, 1, 0, 3) + tuple(range(4, parts.ndim))).reshape((ROWS,) + rest)


def block_order(rows):
    rest = rows.shape[1:]
    parts = rows.reshape((NX, NZ, NY, 4) + rest)
    return jnp.transpose(parts, (2, 1, 0, 3) + tuple(range(4, parts.ndim))).reshape((NY, 128) + rest)


def whole(*shape):
    return pl.BlockSpec(shape, lambda i, m: (0,) * len(shape))


def call(kernel, in_specs, outs, flops, scratch=(), limit=16):
    return pl.pallas_call(
        kernel,
        grid_spec=pltpu.PrefetchScalarGridSpec(
            num_scalar_prefetch=1,
            grid=(1,),
            in_specs=in_specs,
            out_specs=[whole(*out.shape) for out in outs],
            scratch_shapes=scratch,
        ),
        out_shape=outs,
        compiler_params=pltpu.CompilerParams(vmem_limit_bytes=limit << 20),
        cost_estimate=pl.CostEstimate(flops=flops, bytes_accessed=5 << 20, transcendentals=0),
    )


def load_kernel(place_ref, out_ref, held_ref, sems):
    copies = [
        pltpu.make_async_copy(out_ref.at[:, pl.ds(z * 1024, 1024)], held_ref.at[z], sems.at[z]) for z in range(NZ)
    ]
    for copy in copies:
        copy.start()
    for copy in copies:
        copy.wait()


def load(place, teacher_out):
    outs = [jax.ShapeDtypeStruct((NZ, 256, 1024), B16)]
    specs = [pl.BlockSpec(memory_space=pltpu.HBM)]
    return call(load_kernel, specs, outs, 1 << 21, [pltpu.SemaphoreType.DMA((NZ,))], 16)(place, teacher_out)[0]


def teacher_kernel(jobs, place_ref, own_ref, there_ref, held_ref, *parts):
    x = place_ref[2]
    rows = jnp.concatenate([own_ref[...], there_ref[...]], axis=0)
    for k, first, second in jobs:
        columns = pl.ds(pl.multiple_of((k ^ x) * 256, 256), 256)
        for z in range(NZ):
            product = dot(rows, held_ref[z, :, columns], ((1,), (0,))).astype(B16)
            parts[first][z] = product[:64]
            parts[second][z] = product[64:]


def teacher_parts(jobs, place, own, there, held):
    specs = [whole(64, 256), whole(64, 256), whole(NZ, 256, 1024)]
    outs = [jax.ShapeDtypeStruct((NZ, 64, 256), B16)] * (2 * len(jobs))
    flops = 2 * 128 * 256 * 2048 * len(jobs)
    return call(functools.partial(teacher_kernel, jobs), specs, outs, flops, (), 20)(place, own, there, held)


def payload_kernel(place_ref, moved_ref, resid_ref, heads_ref, matches_ref, parts_ref, sent_ref):
    seq = place_ref[1]
    summed = moved_ref[0].astype(F32)
    for z in range(1, NZ):
        summed += moved_ref[z].astype(F32)
    near = resid_ref[pl.ds(pl.multiple_of(seq * 64, 64), 64), :]
    far = resid_ref[pl.ds(pl.multiple_of(64 - seq * 64, 64), 64), :]
    hidden = (jnp.concatenate([near, far], axis=0).astype(F32) + summed).astype(B16)
    matched = jnp.broadcast_to(matches_ref[...].astype(F32), (16, 128)).astype(B16)
    for gs in range(NY):
        sent_ref[gs, 0:128, :] = hidden[:, :128]
        sent_ref[gs, 128:256, :] = hidden[:, 128:]
        sent_ref[gs, 256:384, :] = heads_ref[...]
        sent_ref[gs, 384:400, :] = matched
        sent_ref[gs, 400:432, :] = parts_ref[gs]


def payload(place, moved, resid, heads, matches, parts):
    specs = [whole(NZ, 128, 256), whole(128, 256), whole(128, 128), whole(1, 128), whole(NY, 32, 128)]
    outs = [jax.ShapeDtypeStruct((NY, 432, 128), B16)]
    return call(payload_kernel, specs, outs, 1 << 20)(place, moved, resid, heads, matches, parts)[0]


def gradient_kernel(place_ref, moved_ref, resid_ref, grad_ref):
    total = moved_ref[0].astype(F32)
    for z in range(1, NZ):
        total += moved_ref[z].astype(F32)
    grad = ((resid_ref[...].astype(F32) + total) * 0.125).astype(B16)
    for z in range(NZ):
        grad_ref[z] = grad


def gradient_piece(place, moved, resid):
    outs = [jax.ShapeDtypeStruct((NZ, 64, HALF), B16)]
    specs = [whole(NZ, 64, HALF), whole(64, HALF)]
    return call(gradient_kernel, specs, outs, 1 << 19, (), 8)(place, moved, resid)[0]


def last_kernel(place_ref, back_ref, grad_ref, lines_ref):
    grad = back_ref[0, 0:128, :].astype(F32)
    lines = back_ref[0, 128:144, :].astype(F32)
    for gs in range(1, NY):
        grad += back_ref[gs, 0:128, :].astype(F32)
        lines += back_ref[gs, 128:144, :].astype(F32)
    grad_ref[...] = grad.astype(B16)
    total = jnp.sum(jnp.sum(lines, axis=1, keepdims=True), axis=0, keepdims=True)
    lines_ref[...] = jnp.broadcast_to(total * (64.0 / (ROWS * 8192)), (1, 128))


def last_sums(place, back):
    outs = [jax.ShapeDtypeStruct((128, 128), B16), jax.ShapeDtypeStruct((1, 128), F32)]
    return call(last_kernel, [whole(NY, 144, 128)], outs, 1 << 18)(place, back)


def layout_kernel(place_ref, home_in, other_in, weights_ref):
    weights_ref[0:256, :] = home_in[...]
    weights_ref[256:512, :] = other_in[...]


def layout(place, projector, other):
    specs = [pl.BlockSpec((256, COLS), lambda i, m: (0, m[0])), whole(256, COLS)]
    outs = [jax.ShapeDtypeStruct((512, COLS), B16)]
    return call(layout_kernel, specs, outs, 1 << 21, (), 8)(place, projector, other)[0]


def gather_hidden(place_ref, got_ref, hidden_ref):
    seq = place_ref[1]
    for g in range(4):
        near = pl.ds(pl.multiple_of(g * 128 + seq * 64, 64), 64)
        far = pl.ds(pl.multiple_of(g * 128 + 64 - seq * 64, 64), 64)
        for c in range(2):
            at, home, other = c * 128, slice(c * 128, c * 128 + 128), slice(256 + c * 128, 384 + c * 128)
            hidden_ref[near, home] = got_ref[2 * g + seq, at : at + 64, :]
            hidden_ref[far, home] = got_ref[2 * g + seq, at + 64 : at + 128, :]
            hidden_ref[far, other] = got_ref[2 * g + 1 - seq, at : at + 64, :]
            hidden_ref[near, other] = got_ref[2 * g + 1 - seq, at + 64 : at + 128, :]


def combine_kernel(jobs, place_ref, picked_ref, got_ref, heads_ref, out_ref, weights_ref, *refs):
    x = place_ref[2]
    parts, hidden_ref = refs[:-1], refs[-1]
    gather_hidden(place_ref, got_ref, hidden_ref)
    row = lax.broadcasted_iota(jnp.int32, (512, 256), 0)
    for k, halves in jobs:
        choose = (row == picked_ref[k ^ x]).astype(F32).astype(B16)
        selected = dot(choose, hidden_ref[...], ((0,), (0,))).astype(B16)
        heads = heads_ref[k ^ x]
        for half, to in halves:
            columns = slice(half * HALF, (half + 1) * HALF)
            total = dot(heads, out_ref[:, columns], ((1,), (0,)))
            total -= dot(selected, weights_ref[:, columns], ((1,), (0,)))
            parts[to][...] = total.astype(B16)


FAR = ((2, ((0, 0), (1, 1))),)
REST = ((1, ((0, 0), (1, 3))), (3, ((1, 4), (0, 1))), (0, ((0, 2), (1, 5))))


def combined_parts(jobs, place, picked, got, heads, student_out, weights):
    block = pl.BlockSpec((128, COLS), lambda i, m: (0, m[0]))
    specs = [whole(NX, 1, 256), whole(NY, 432, 128), whole(NX, 256, 128), block, whole(512, COLS)]
    count = sum(len(halves) for _, halves in jobs)
    outs = [jax.ShapeDtypeStruct((256, HALF), B16)] * count
    return call(
        functools.partial(combine_kernel, jobs), specs, outs, count * 2 * 256 * 512 * 900, [pltpu.VMEM((512, 512), B16)], 16
    )(place, picked, got, heads, student_out, weights)


def final_kernel(place_ref, *refs):
    x = place_ref[2]
    first, second = refs[:4], refs[4:8]
    out_ref, heads_ref, part_ref, squares_ref, weight_ref, sums_ref = refs[8:]
    left = jnp.zeros((128, HALF), F32)
    right = jnp.zeros((128, HALF), F32)
    for k in range(NX):
        near, far = first[k][...], second[k][...]
        part = dot(near, out_ref[:, :HALF], ((1,), (1,))) + dot(far, out_ref[:, HALF:], ((1,), (1,)))
        part_ref[k ^ x] = part.astype(B16)
        heads = heads_ref[k ^ x]
        left += dot(heads, near, ((0,), (0,)))
        right += dot(heads, far, ((0,), (0,)))
        near, far = near.astype(F32), far.astype(F32)
        line = jnp.sum(near * near + far * far, axis=0, keepdims=True)
        sums_ref[k ^ x] = line[:, :128] + line[:, 128:256] + line[:, 256:384] + line[:, 384:]
    weight_ref[:, :HALF] = left.astype(B16)
    weight_ref[:, HALF:] = right.astype(B16)
    total = sums_ref[0] + sums_ref[1] + sums_ref[2] + sums_ref[3]
    top = total.astype(B16).astype(F32)
    middle = (total - top).astype(B16).astype(F32)
    bottom = total - top - middle
    row = lax.broadcasted_iota(jnp.int32, (16, 128), 0)
    lines = jnp.where(row == 0, top, jnp.where(row == 1, middle, jnp.where(row == 2, bottom, 0.0)))
    squares_ref[...] = lines.astype(B16)


def final_parts(place, gathered, student_out, heads):
    specs = [whole(256, HALF)] * 8 + [pl.BlockSpec((128, COLS), lambda i, m: (0, m[0])), whole(NX, 256, 128)]
    outs = [
        jax.ShapeDtypeStruct((NX, 256, 128), B16),
        jax.ShapeDtypeStruct((16, 128), B16),
        jax.ShapeDtypeStruct((128, COLS), B16),
    ]
    return call(final_kernel, specs, outs, 2 * 1024 * 1024 * 256, [pltpu.VMEM((NX, 1, 128), F32)])(
        place, *gathered, student_out, heads
    )


def local(
    teacher_heads,
    teacher_out,
    teacher_resid,
    matches,
    projector,
    student_heads,
    student_out,
    student_resid,
):
    seq = lax.axis_index("seq")
    member = lax.axis_index(COLUMN)
    place = jnp.stack([member, seq, lax.axis_index("x")]).astype(jnp.int32)
    swap = [(0, 1), (1, 0)]

    there = lax.ppermute(teacher_heads, "seq", swap)
    held = load(place, teacher_out)
    jobs = ((2, 2, 6), (1, 1, 5), (3, 3, 7), (0, 0, 4))
    parts = list(teacher_parts(jobs, place, teacher_heads, there, held))
    first, second = parts[:NX], parts[NX:]

    second[0], later = lax.optimization_barrier((second[0], member))
    away = lax.dynamic_slice(projector, (0, (later + 1 - 2 * seq) * COLS), (256, COLS))
    other = lax.ppermute(away, "seq", swap)

    summed, other = reduce_x(first, second, (away,), (other,))
    moved = lax.all_to_all(summed, "z", 0, 0)
    own_matches = lax.dynamic_slice(matches, (seq * 128,), (128,)).astype(B16)
    resid_parts = jnp.transpose(student_resid.reshape(4, NY, 8, 128), (1, 0, 2, 3)).reshape(NY, 32, 128)
    sent = payload(place, moved, teacher_resid, student_heads, own_matches.reshape(1, 128), resid_parts)
    spot, sent = lax.optimization_barrier((place, sent))
    weights = layout(spot, projector, other)
    got = lax.all_to_all(sent, COLUMN, 0, 0)
    heads = own_order(got[:, 256:384]).reshape(NX, 256, 128)
    base = (jnp.arange(NY, dtype=jnp.int32) // 2 * 128)[:, None]
    picked = own_order(got[:, 384].astype(jnp.int32) + base).reshape(NX, 1, 256)
    operands = (place, picked, got, heads, student_out, weights)
    far = [part.reshape(NZ, 32, HALF) for part in combined_parts(FAR, *operands)]
    rest = [part.reshape(NZ, 32, HALF) for part in combined_parts(REST, *operands)]
    resid = got[:, 400:].reshape(32, 2, HALF)
    resid = jnp.concatenate([resid[:, 0], resid[:, 1]], axis=0)
    (summed,) = reduce_x((rest[2], rest[0], far[0], rest[1]), (rest[5], rest[3], far[1], rest[4]), ())
    moved = lax.all_to_all(summed, "z", 0, 0)
    grad = gradient_piece(place, moved, resid)

    tall = lax.all_to_all(grad, "z", 0, 0)
    gathered = gather_x(tall[:, :32].reshape(256, HALF), tall[:, 32:].reshape(256, HALF))

    heads_part, squares, grad_weight = final_parts(place, gathered, student_out, heads)
    sent = jnp.concatenate(
        [block_order(heads_part.reshape(ROWS, 128)), jnp.broadcast_to(squares[None], (NY, 16, 128))], axis=1
    )
    back = lax.all_to_all(sent, COLUMN, 0, 0)
    grad_heads, loss = last_sums(place, back)
    loss = loss[0, :1]
    return (loss, grad_heads, grad_weight)


def solution(mesh):
    cut = Mesh(mesh.devices.reshape(2, 2, 2, NZ, NX), COLUMN + PLANE)
    every = COLUMN + PLANE
    return jax.shard_map(
        local,
        mesh=cut,
        in_specs=(
            P(COLUMN, PLANE),
            P(PLANE, "seq"),
            P(GROUP, ("seq",) + PLANE),
            P(GROUP),
            P(("seq",) + PLANE, None),
            P(COLUMN, PLANE),
            P(PLANE, None),
            P(every, None),
        ),
        out_specs=(P(), P(COLUMN, PLANE), P(PLANE, COLUMN)),
        check_vma=False,
    )
```
